32 devices in a mesh: section: 2 (over y), fsdp: 4 (over z), dp: 4 (over x, core).
Axes of the slice: x: 2, y: 2, z: 4, core: 2. Of those that a mesh axis runs over, the one named last changes fastest.
Arguments:
- latents: bfloat16 [32, 256, 768], P(('fsdp', 'dp')), may hold values from -6 to 6
- cotangent: bfloat16 [32, 256, 768], P(('fsdp', 'dp')), may hold values from -6 to 6
- timesteps: int32 [32], P(('fsdp', 'dp')), may hold values from 0 to 999
- classes: int32 [32], P(('fsdp', 'dp')), may hold values from 0 to 999
- modulation: bfloat16 [2, 768, 4608], P('section', 'fsdp'), may hold values from -0.21875 to 0.21875
- inward: bfloat16 [2, 768, 2304], P('section', 'fsdp'), may hold values from -0.21875 to 0.21875
- outward: bfloat16 [2, 768, 768], P('section', 'fsdp'), may hold values from -0.875 to 0.875
- widen: bfloat16 [2, 768, 3072], P('section', 'fsdp'), may hold values from -0.21875 to 0.21875
- narrow: bfloat16 [2, 3072, 768], P('section', 'fsdp'), may hold values from -0.109375 to 0.109375
- biases: bfloat16 [2, 10752], P('section', 'fsdp'), may hold values from -3 to 3
- class_table: bfloat16 [1000, 768], P('fsdp'), may hold values from -6 to 6
Outputs:
- section_outputs: bfloat16 [2, 32, 256, 768], P('section', ('fsdp', 'dp'))
- input_gradients: bfloat16 [2, 32, 256, 768], P('section', ('fsdp', 'dp'))
- gradient_modulation: float32 [2, 768, 4608], P('section', 'fsdp')
- gradient_inward: float32 [2, 768, 2304], P('section', 'fsdp')
- gradient_outward: float32 [2, 768, 768], P('section', 'fsdp')
- gradient_widen: float32 [2, 768, 3072], P('section', 'fsdp')
- gradient_narrow: float32 [2, 3072, 768], P('section', 'fsdp')
- gradient_biases: float32 [2, 10752], P('section', 'fsdp')
- gradient_table: float32 [1000, 768], P('fsdp')
The draws below stay inside these ranges and needn't reach their ends.
All inputs are finite; a program needn't handle non-finite values.
Results may differ from the reference program's by a relative error of at most 0.02.
Values may be sent and summed in bfloat16 or wider, within the bound.
No kernel may reach another device: no remote copies, remote signals or barrier semaphores. Data moves between devices by JAX's collectives and lax.ppermute only.
A program may use at most 256 MiB of HBM per device.

```python
import math
import jax
import jax.numpy as jnp
from jax import lax

D = 768
HEADS = 12
HEAD = 64
FF = 3072
NCLASS = 1000
LEN = 256
LATENTS = 32
BIAS_W = 10752


def plant(drawn, stream_key, low, largest):
    longest = drawn.shape.index(max(drawn.shape))
    spots = []
    for shift in (0, 1):
        where = [jax.random.randint(jax.random.fold_in(stream_key, axis), (), 0, length) for axis, length in enumerate(drawn.shape)]
        where[longest] = (where[longest] + shift) % drawn.shape[longest]
        spots.append(tuple(where))
    return drawn.at[spots[0]].set(low).at[spots[1]].set(largest)


def strengthened(array, key, source, target, blocks, factor):
    owner, partner = [(jnp.arange(array.shape[dim]) // (array.shape[dim] // blocks)).reshape([-1 if axis == dim else 1 for axis in range(array.ndim)]) for dim in (source, target)]
    chosen = jax.random.permutation(key, blocks)[partner]
    strong = (owner == chosen) | (owner == (partner + blocks // 2) % blocks)
    return jnp.where(strong, factor * array, array)


def steps_of(key, shape, cuts, low, high):
    gain, own = 1.0, jax.random.fold_in(key, 6)
    for dim, shards_of in cuts:
        heights = jnp.exp(jax.random.uniform(jax.random.fold_in(own, dim), (shards_of,), jnp.float32, low / len(cuts), high / len(cuts)))
        gain = gain * jnp.repeat(heights, shape[dim] // shards_of).reshape([-1 if axis == dim else 1 for axis in range(len(shape))])
    return gain


def normal_values(rng, extent, scale, bound, cuts=(), held_as=jnp.bfloat16):
    result = scale * jax.random.normal(rng, extent, jnp.float32)
    if cuts:
        result = result * steps_of(rng, extent, cuts, -0.22, 0.18)
    return jnp.clip(result, -bound, bound).astype(held_as)


def gaussian_with(own_key, dims, spread, most, cuts, heavy, kind=jnp.bfloat16):
    result = spread * jax.random.normal(own_key, dims, jnp.float32)
    if cuts:
        result = result * steps_of(own_key, dims, cuts, -0.22, 0.18)
    return jnp.clip(strengthened(result, jax.random.fold_in(own_key, 3), *heavy), -most, most).astype(kind)


def setup_inputs(seed: int = 0) -> dict:
    splits = jax.random.split(jax.random.key(seed), 12)
    return {
        "latents": gaussian_with(splits[0], (LATENTS, LEN, D), 1.0, 6.0, ((0, 16),), (0, 2, 16, 2.0)),
        "cotangent": gaussian_with(splits[1], (LATENTS, LEN, D), 1.0, 6.0, ((0, 16),), (0, 2, 16, 2.0)),
        "timesteps": plant(jax.random.randint(splits[2], (LATENTS,), 0, 1000), jax.random.fold_in(splits[2], 1), 0, 999).astype(jnp.int32),
        "classes": plant(jax.random.randint(splits[3], (LATENTS,), 0, NCLASS), jax.random.fold_in(splits[3], 1), 0, NCLASS - 1).astype(jnp.int32),
        "modulation": normal_values(splits[4], (2, D, 6 * D), D ** -0.5, 0.21875, ((0, 2), (1, 4))),
        "inward": normal_values(splits[5], (2, D, 3 * D), D ** -0.5, 0.21875, ((0, 2), (1, 4))),
        "outward": normal_values(splits[6], (2, D, D), (D // 16) ** -0.5, 0.875, ((0, 2), (1, 4))),
        "widen": normal_values(splits[7], (2, D, FF), D ** -0.5, 0.21875, ((0, 2), (1, 4))),
        "narrow": normal_values(splits[8], (2, FF, D), FF ** -0.5, 0.109375, ((0, 2), (1, 4))),
        "biases": normal_values(splits[9], (2, BIAS_W), 0.5, 3.0, ((0, 2), (1, 4))),
        "class_table": normal_values(splits[10], (NCLASS, D), 1.0, 6.0, ((0, 4),)),
    }


@jax.custom_vjp
def reduced_copy(v):
    return lax.optimization_barrier(v.astype(jnp.bfloat16)).astype(jnp.float32)

@jax.custom_vjp
def low_back(v):
    return v

def low_keep(v):
    return (reduced_copy(v), None)

def low_pass(kept, grad):
    return (grad,)

def back_keep(v):
    return (v, None)

def back_low(kept, grad):
    return (reduced_copy(grad),)
reduced_copy.defvjp(low_keep, low_pass)
low_back.defvjp(back_keep, back_low)
eps = 1e-06

def product(left, right):
    return jnp.dot(left, right, precision=lax.Precision.HIGHEST)

def normalize(values):
    average = lax.optimization_barrier(jnp.mean(values, axis=-1, keepdims=True))
    centred = values - average
    variance = lax.optimization_barrier(jnp.mean(centred * centred, axis=-1, keepdims=True))
    return centred * lax.rsqrt(variance + eps)

def timestep_features(step_ids, model_width):
    half_width = model_width // 2
    frequencies = jnp.exp(-math.log(10000.0) * jnp.arange(half_width, dtype=jnp.float32) / half_width)
    angles = step_ids.astype(jnp.float32)[:, None] * frequencies[None, :]
    return jnp.concatenate([jnp.cos(angles), jnp.sin(angles)], axis=-1)

def diffusion_transformer_block(residual_state, condition_reduced_precision, modulation, inward, outward, widen, narrow, every_bias):
    group_size, length, model_width = residual_state.shape
    hidden_units = widen.shape[1]
    modulated = low_back(product(condition_reduced_precision, modulation) + every_bias[:6 * model_width])
    pieces = jnp.split(modulated, 6, axis=-1)
    first_normed = normalize(residual_state) * (1.0 + pieces[1][:, None]) + pieces[0][:, None]
    input_bias = jnp.concatenate([every_bias[6 * model_width:7 * model_width], jnp.zeros((model_width,), jnp.float32), every_bias[7 * model_width:8 * model_width]])
    projected = reduced_copy(low_back(product(reduced_copy(first_normed), inward) + input_bias))
    heads_view = projected.reshape(group_size, length, 3, HEADS, HEAD)
    scores = low_back(jnp.einsum('blhd,bmhd->bhlm', heads_view[:, :, 0], heads_view[:, :, 1], precision=lax.Precision.HIGHEST) * HEAD ** (-0.5))
    weights_soft = reduced_copy(jax.nn.softmax(scores, axis=-1))
    attended = reduced_copy(low_back(jnp.einsum('bhlm,bmhd->blhd', weights_soft, heads_view[:, :, 2], precision=lax.Precision.HIGHEST).reshape(group_size, length, model_width)))
    attention_branch = low_back(product(attended, outward) + every_bias[8 * model_width:9 * model_width])
    middle = residual_state + pieces[2][:, None] * attention_branch
    second_normed = normalize(middle) * (1.0 + pieces[4][:, None]) + pieces[3][:, None]
    hidden = low_back(product(reduced_copy(second_normed), widen) + every_bias[9 * model_width:9 * model_width + hidden_units])
    activated = reduced_copy(jax.nn.gelu(hidden, approximate=True))
    feedforward = low_back(product(activated, narrow) + every_bias[9 * model_width + hidden_units:])
    return middle + pieces[5][:, None] * feedforward

def reference(latents, cotangent, timesteps, classes, modulation, inward, outward, widen, narrow, biases, class_table):
    group_size = math.gcd(LATENTS, max(1, 4096 // LEN))
    group_count = LATENTS // group_size

    def grouped(values):
        return values.reshape((group_count, group_size) + values.shape[1:])

    def forward_pass(inputs_all, probe_zero, every_modulation, every_inward, every_outward, every_widen, every_narrow, every_bias, class_rows):
        condition = timestep_features(timesteps, D) + jnp.take(class_rows, classes, axis=0)
        condition_reduced_precision = reduced_copy(jax.nn.silu(condition))

        def one_group(members):
            residual_state, probe_part, condition_slice = members
            first_result = reduced_copy(diffusion_transformer_block(residual_state, condition_slice, every_modulation[0], every_inward[0], every_outward[0], every_widen[0], every_narrow[0], every_bias[0]))
            block_entry = low_back(first_result + probe_part)
            second_result = diffusion_transformer_block(block_entry, condition_slice, every_modulation[1], every_inward[1], every_outward[1], every_widen[1], every_narrow[1], every_bias[1])
            return (first_result, second_result)
        first_result, second_result = lax.map(jax.checkpoint(one_group), (grouped(inputs_all), grouped(probe_zero), grouped(condition_reduced_precision)))
        return (first_result.reshape(inputs_all.shape), second_result.reshape(inputs_all.shape))
    floats = [latents.astype(jnp.float32), jnp.zeros(latents.shape, jnp.float32)]
    floats = floats + [member.astype(jnp.float32) for member in (modulation, inward, outward, widen, narrow, biases, class_table)]
    outputs, pullback = jax.vjp(forward_pass, *floats)
    gradients = pullback((jnp.zeros_like(outputs[0]), cotangent.astype(jnp.float32)))
    section_outputs = jnp.stack([outputs[0], outputs[1]]).astype(jnp.bfloat16)
    input_gradients = jnp.stack([gradients[0], gradients[1]]).astype(jnp.bfloat16)
    return (section_outputs, input_gradients, gradients[2], gradients[3], gradients[4], gradients[5], gradients[6], gradients[7], gradients[8])
```

```python
import math

import jax
import jax.numpy as jnp
from jax import lax
from jax.sharding import PartitionSpec as P

HEADS = 12

eps = 1e-06
f32 = jnp.float32
bf16 = jnp.bfloat16


def dot(left, right, dims):
    return lax.dot_general(left, right, (dims, ((), ())), preferred_element_type=f32)


def normalize(values):
    average = jnp.mean(values, axis=-1, keepdims=True)
    centred = values - average
    variance = jnp.mean(centred * centred, axis=-1, keepdims=True)
    inverse = lax.rsqrt(variance + eps)
    return (centred * inverse, inverse)


def normal_back(grad_normed, normed, inverse):
    first_mean = jnp.mean(grad_normed, axis=-1, keepdims=True)
    cross_mean = jnp.mean(grad_normed * normed, axis=-1, keepdims=True)
    return inverse * (grad_normed - first_mean - normed * cross_mean)


def timestep_features(step_ids, model_width):
    half_width = model_width // 2
    frequencies = jnp.exp(
        -math.log(10000.0) * jnp.arange(half_width, dtype=f32) / half_width
    )
    angles = step_ids[:, None] * frequencies[None, :]
    return jnp.concatenate([jnp.cos(angles), jnp.sin(angles)], axis=-1)


def gelu_and_slope(hidden):
    c = math.sqrt(2.0 / math.pi)
    squared = hidden * hidden
    t = jnp.tanh(c * hidden * (1.0 + 0.044715 * squared))
    value = 0.5 * hidden * (1.0 + t)
    slope = 0.5 * (1.0 + t) + 0.5 * hidden * (1.0 - t * t) * c * (1.0 + 3 * 0.044715 * squared)
    return value, slope


def forward_block(x_in, pieces, params, bias):
    inward, outward, widen, narrow = params
    batch, length, width = x_in.shape
    head = width // HEADS
    x = x_in.astype(f32)
    first_norm, first_inverse = normalize(x)
    first_low = (first_norm * (1.0 + pieces[1][:, None]) + pieces[0][:, None]).astype(bf16)
    projected = (
        jnp.einsum("bli,ij->blj", first_low, inward, preferred_element_type=f32) + bias["in"]
    ).astype(bf16)
    view = projected.reshape(batch, length, 3, HEADS, head)
    scores = jnp.einsum(
        "blhd,bmhd->bhlm", view[:, :, 0], view[:, :, 1], preferred_element_type=f32
    ) * head ** (-0.5)
    soft = jax.nn.softmax(scores, axis=-1)
    rounded = soft.astype(bf16)
    attended = jnp.einsum("bhlm,bmhd->blhd", rounded, view[:, :, 2], preferred_element_type=f32)
    attended = attended.reshape(batch, length, width).astype(bf16)
    branch = jnp.einsum("bli,ij->blj", attended, outward, preferred_element_type=f32) + bias["out"]
    middle = x + pieces[2][:, None] * branch
    second_norm, second_inverse = normalize(middle)
    second_low = (second_norm * (1.0 + pieces[4][:, None]) + pieces[3][:, None]).astype(bf16)
    hidden = jnp.einsum("bli,ij->blj", second_low, widen, preferred_element_type=f32) + bias["ff1"]
    value, slope = gelu_and_slope(hidden)
    activated = value.astype(bf16)
    feed = jnp.einsum("bli,ij->blj", activated, narrow, preferred_element_type=f32) + bias["ff2"]
    result = (middle + pieces[5][:, None] * feed).astype(bf16)
    saved = dict(
        x_norm=first_norm, x_inverse=first_inverse, first_low=first_low, projected=projected,
        soft=soft, rounded=rounded, attended=attended, branch=branch, m_norm=second_norm,
        m_inverse=second_inverse, second_low=second_low, slope=slope.astype(bf16),
        activated=activated, feed=feed,
    )
    return result, saved


def backward_block(grad_in, saved, pieces, params, weights_too):
    inward, outward, widen, narrow = params
    batch, length, width = grad_in.shape
    head = width // HEADS
    factor = head ** (-0.5)
    grad_out = grad_in.astype(f32)
    out = {}

    def weight(a, g):
        return jnp.einsum("bli,blj->ij", a, g, preferred_element_type=f32)

    feed_grad = (pieces[5][:, None] * grad_out).astype(bf16)
    if weights_too:
        out["narrow"] = weight(saved["activated"], feed_grad)
    hidden_grad = (
        jnp.einsum("blj,ij->bli", feed_grad, narrow, preferred_element_type=f32)
        * saved["slope"].astype(f32)
    ).astype(bf16)
    if weights_too:
        out["widen"] = weight(saved["second_low"], hidden_grad)
    second_grad = jnp.einsum("blj,ij->bli", hidden_grad, widen, preferred_element_type=f32)
    middle_grad = grad_out + normal_back(
        second_grad * (1.0 + pieces[4][:, None]), saved["m_norm"], saved["m_inverse"]
    )
    attention_grad = (pieces[2][:, None] * middle_grad).astype(bf16)
    if weights_too:
        out["outward"] = weight(saved["attended"], attention_grad)
    attended_grad = jnp.einsum("blj,ij->bli", attention_grad, outward, preferred_element_type=f32)
    attended_grad = attended_grad.astype(bf16).reshape(batch, length, HEADS, head)
    view = saved["projected"].reshape(batch, length, 3, HEADS, head)
    value_grad = jnp.einsum(
        "bhlm,blhd->bmhd", saved["rounded"], attended_grad, preferred_element_type=f32
    )
    weight_grad = jnp.einsum(
        "blhd,bmhd->bhlm", attended_grad, view[:, :, 2], preferred_element_type=f32
    )
    soft = saved["soft"]
    score_grad = soft * (weight_grad - jnp.sum(weight_grad * soft, axis=-1, keepdims=True))
    score_grad = score_grad.astype(bf16)
    query_grad = (
        jnp.einsum("bhlm,bmhd->blhd", score_grad, view[:, :, 1], preferred_element_type=f32)
        * factor
    )
    key_grad = (
        jnp.einsum("bhlm,blhd->bmhd", score_grad, view[:, :, 0], preferred_element_type=f32)
        * factor
    )
    projected_grad = jnp.concatenate(
        [g.astype(bf16).reshape(batch, length, width) for g in (query_grad, key_grad, value_grad)],
        axis=-1,
    )
    if weights_too:
        out["inward"] = weight(saved["first_low"], projected_grad)
    first_grad = jnp.einsum("blj,ij->bli", projected_grad, inward, preferred_element_type=f32)
    stream = middle_grad + normal_back(
        first_grad * (1.0 + pieces[1][:, None]), saved["x_norm"], saved["x_inverse"]
    )
    if weights_too:
        total = jnp.sum(projected_grad.astype(f32), axis=(0, 1))
        out["biases"] = jnp.concatenate(
            [
                total[:width],
                total[2 * width :],
                jnp.sum(attention_grad.astype(f32), axis=(0, 1)),
                jnp.sum(hidden_grad.astype(f32), axis=(0, 1)),
                jnp.sum(feed_grad.astype(f32), axis=(0, 1)),
            ]
        )
        out["modulated"] = jnp.concatenate(
            [
                jnp.sum(first_grad, axis=1),
                jnp.sum(first_grad * saved["x_norm"], axis=1),
                jnp.sum(middle_grad * saved["branch"], axis=1),
                jnp.sum(second_grad, axis=1),
                jnp.sum(second_grad * saved["m_norm"], axis=1),
                jnp.sum(grad_out * saved["feed"], axis=1),
            ],
            axis=-1,
        ).astype(bf16)
    return stream.astype(bf16), out


def pick(array, index):
    return lax.dynamic_index_in_dim(array, index, 0, keepdims=False)


def swap(array, bit, count):
    return lax.ppermute(array, "dp", [(i, i ^ (1 << bit)) for i in range(count)])


def reduce_weight(grad, fsdp, dp, d, f):
    bits = dp.bit_length() - 1
    rows, columns = grad.shape
    share = rows // (fsdp * dp)
    held = grad.astype(bf16).reshape((fsdp, dp, share, columns))
    held = jnp.swapaxes(held, 0, 1)
    for bit in range(bits):
        mine = (d >> bit) & 1
        held = held.reshape((held.shape[0] // 2, 2) + held.shape[1:])
        held = jnp.moveaxis(held, 1, 0)
        got = swap(pick(held, 1 - mine), bit, dp)
        held = (pick(held, mine).astype(f32) + got.astype(f32)).astype(bf16)
    held = held[0]
    total = pick(held, f).astype(f32)
    for step in range(1, fsdp):
        sent = pick(held, lax.rem(f + step, fsdp))
        total += lax.ppermute(
            sent, "fsdp", [(i, (i + step) % fsdp) for i in range(fsdp)]
        ).astype(f32)
    whole = total.astype(bf16)[None]
    for bit in reversed(range(bits)):
        mine = (d >> bit) & 1
        got = swap(whole, bit, dp)
        low = jnp.where(mine == 0, whole, got)
        high = jnp.where(mine == 0, got, whole)
        whole = jnp.stack([low, high], axis=1).reshape((-1,) + whole.shape[1:])
    return whole.reshape((rows // fsdp, columns)).astype(f32)


def per_device(
    latents, cotangent, timesteps, classes,
    modulation, inward, outward, widen, narrow, biases, class_table,
):
    section_zero = lax.axis_index("section") == 0
    fsdp, dp = lax.axis_size("fsdp"), lax.axis_size("dp")
    f, d = lax.axis_index("fsdp"), lax.axis_index("dp")
    batch, length, width = latents.shape
    table_rows = class_table.shape[0]
    slice_width = modulation.shape[1]
    bias_share = biases.shape[1]
    hidden_units = widen.shape[2]

    def gather(shard):
        rows = shard.shape[1] // dp
        own = lax.dynamic_slice_in_dim(shard[0], d * rows, rows, 0)
        return lax.all_gather(own, ("fsdp", "dp"), axis=0, tiled=True)

    small = jnp.concatenate([biases[0].astype(f32), timesteps.astype(f32), classes.astype(f32)])
    small = lax.all_gather(small, ("fsdp", "dp"), axis=0)
    every_bias = small.reshape(fsdp, dp, -1)[:, 0, :bias_share].reshape(-1)
    steps = small[:, bias_share : bias_share + batch].reshape(-1)
    ids = small[:, bias_share + batch :].reshape(-1).astype(jnp.int32)
    labels = f * table_rows + jnp.arange(table_rows, dtype=jnp.int32)
    onehot = (ids[:, None] == labels[None, :]).astype(bf16)
    rows = lax.psum(dot(onehot, class_table, ((1,), (0,))).astype(bf16), "fsdp")
    condition = timestep_features(steps, width) + rows.astype(f32)
    condition_low = jax.nn.silu(condition).astype(bf16)
    low_slice = lax.dynamic_slice_in_dim(condition_low, f * slice_width, slice_width, 1)
    group = lax.dynamic_index_in_dim(
        low_slice.reshape(fsdp, dp, batch, slice_width), d, 1, keepdims=False
    )
    partial = dot(group.reshape(fsdp * batch, slice_width), modulation[0], ((1,), (0,)))
    partial = partial.reshape(fsdp, batch, -1)
    modulated = jnp.sum(lax.all_to_all(partial, "fsdp", 0, 0), axis=0) + every_bias[: 6 * width]
    pieces = jnp.split(modulated, 6, axis=-1)
    bias = {
        "in": jnp.concatenate(
            [
                every_bias[6 * width : 7 * width],
                jnp.zeros((width,), f32),
                every_bias[7 * width : 8 * width],
            ]
        ),
        "out": every_bias[8 * width : 9 * width],
        "ff1": every_bias[9 * width : 9 * width + hidden_units],
        "ff2": every_bias[9 * width + hidden_units :],
    }
    params = (gather(inward), gather(outward), gather(widen), gather(narrow))

    first, unused = forward_block(latents, pieces, params, bias)
    incoming = lax.ppermute(first, "section", [(0, 1)])
    block_in = jnp.where(section_zero, latents, incoming)
    section_output, saved = forward_block(block_in, pieces, params, bias)
    early, unused = backward_block(cotangent, saved, pieces, params, False)
    returning = lax.ppermute(early, "section", [(1, 0)])
    grad_in = jnp.where(section_zero, returning, cotangent)
    input_gradient, grads = backward_block(grad_in, saved, pieces, params, True)

    shares = {
        name: reduce_weight(grads[name], fsdp, dp, d, f)
        for name in ("narrow", "widen", "outward", "inward")
    }
    tail = jnp.concatenate([grads["modulated"].reshape(-1), grads["biases"].astype(bf16)])
    tail = lax.all_gather(tail, ("fsdp", "dp"), axis=0)
    count = batch * 6 * width
    modulated_grad = tail[:, :count].reshape(-1, 6 * width)
    bias_grad = jnp.concatenate(
        [
            jnp.sum(modulated_grad.astype(f32), axis=0),
            jnp.sum(tail[:, count:].astype(f32), axis=0),
        ]
    )
    bias_grad = lax.dynamic_slice_in_dim(bias_grad, f * bias_share, bias_share, 0)
    modulation_grad = dot(low_slice, modulated_grad, ((0,), (0,)))
    condition_grad = dot(modulated_grad, modulation[0], ((1,), (1,)))
    condition_grad = lax.all_gather(condition_grad, ("section", "fsdp"), axis=0)
    condition_grad = jnp.sum(condition_grad.reshape((-1, fsdp) + condition_grad.shape[1:]), axis=0)
    condition_grad = jnp.swapaxes(condition_grad, 0, 1).reshape(-1, width)
    gate = jax.nn.sigmoid(condition)
    condition_grad = condition_grad * (gate * (1.0 + condition * (1.0 - gate)))
    table_grad = lax.dot_general(
        onehot.astype(f32), condition_grad, (((0,), (0,)), ((), ())),
        precision=lax.Precision.HIGHEST,
    )
    return (
        section_output[None],
        input_gradient[None],
        modulation_grad[None],
        shares["inward"][None],
        shares["outward"][None],
        shares["widen"][None],
        shares["narrow"][None],
        bias_grad[None],
        table_grad,
    )


def solution(mesh):
    return jax.shard_map(
        per_device,
        mesh=mesh,
        in_specs=(
            P(("fsdp", "dp"), None, None),
            P(("fsdp", "dp"), None, None),
            P(("fsdp", "dp")),
            P(("fsdp", "dp")),
            P("section", "fsdp", None),
            P("section", "fsdp", None),
            P("section", "fsdp", None),
            P("section", "fsdp", None),
            P("section", "fsdp", None),
            P("section", "fsdp"),
            P("fsdp", None),
        ),
        out_specs=(
            P("section", ("fsdp", "dp"), None, None),
            P("section", ("fsdp", "dp"), None, None),
            P("section", "fsdp", None),
            P("section", "fsdp", None),
            P("section", "fsdp", None),
            P("section", "fsdp", None),
            P("section", "fsdp", None),
            P("section", "fsdp"),
            P("fsdp", None),
        ),
        check_vma=False,
    )
```

```python
import math

import jax
import jax.numpy as jnp
from jax import lax
from jax.experimental import pallas as pl
from jax.experimental.pallas import tpu as pltpu
from jax.sharding import PartitionSpec as P

HEADS = 12

eps = 1e-06
f32 = jnp.float32
bf16 = jnp.bfloat16


def dot(left, right, dims):
    return lax.dot_general(left, right, (dims, ((), ())), preferred_element_type=f32)


def normalize(values):
    average = jnp.mean(values, axis=-1, keepdims=True)
    centred = values - average
    variance = jnp.mean(centred * centred, axis=-1, keepdims=True)
    inverse = lax.rsqrt(variance + eps)
    return (centred * inverse, inverse)


def normal_back(grad_normed, normed, inverse):
    first_mean = jnp.mean(grad_normed, axis=-1, keepdims=True)
    cross_mean = jnp.mean(grad_normed * normed, axis=-1, keepdims=True)
    return inverse * (grad_normed - first_mean - normed * cross_mean)


def timestep_features(step_ids, model_width):
    half_width = model_width // 2
    frequencies = jnp.exp(
        -math.log(10000.0) * jnp.arange(half_width, dtype=f32) / half_width
    )
    angles = step_ids[:, None] * frequencies[None, :]
    return jnp.concatenate([jnp.cos(angles), jnp.sin(angles)], axis=-1)


def gelu_and_slope(hidden):
    c = math.sqrt(2.0 / math.pi)
    squared = hidden * hidden
    t = jnp.tanh(c * hidden * (1.0 + 0.044715 * squared))
    value = 0.5 * hidden * (1.0 + t)
    slope = 0.5 * (1.0 + t) + 0.5 * hidden * (1.0 - t * t) * c * (1.0 + 3 * 0.044715 * squared)
    return value, slope


def forward_block(x_in, pieces, params, bias):
    inward, outward, widen, narrow = params
    batch, length, width = x_in.shape
    head = width // HEADS
    x = x_in.astype(f32)
    first_norm, first_inverse = normalize(x)
    first_low = (first_norm * (1.0 + pieces[1][:, None]) + pieces[0][:, None]).astype(bf16)
    projected = (
        jnp.einsum("bli,ij->blj", first_low, inward, preferred_element_type=f32) + bias["in"]
    ).astype(bf16)
    view = projected.reshape(batch, length, 3, HEADS, head)
    scores = jnp.einsum(
        "blhd,bmhd->bhlm", view[:, :, 0], view[:, :, 1], preferred_element_type=f32
    ) * head ** (-0.5)
    soft = jax.nn.softmax(scores, axis=-1)
    rounded = soft.astype(bf16)
    attended = jnp.einsum("bhlm,bmhd->blhd", rounded, view[:, :, 2], preferred_element_type=f32)
    attended = attended.reshape(batch, length, width).astype(bf16)
    branch = jnp.einsum("bli,ij->blj", attended, outward, preferred_element_type=f32) + bias["out"]
    middle = x + pieces[2][:, None] * branch
    second_norm, second_inverse = normalize(middle)
    second_low = (second_norm * (1.0 + pieces[4][:, None]) + pieces[3][:, None]).astype(bf16)
    hidden = jnp.einsum("bli,ij->blj", second_low, widen, preferred_element_type=f32) + bias["ff1"]
    value, slope = gelu_and_slope(hidden)
    activated = value.astype(bf16)
    feed = jnp.einsum("bli,ij->blj", activated, narrow, preferred_element_type=f32) + bias["ff2"]
    result = (middle + pieces[5][:, None] * feed).astype(bf16)
    saved = dict(
        x_norm=first_norm, x_inverse=first_inverse, first_low=first_low, projected=projected,
        soft=soft, rounded=rounded, attended=attended, branch=branch, m_norm=second_norm,
        m_inverse=second_inverse, second_low=second_low, slope=slope.astype(bf16),
        activated=activated, feed=feed,
    )
    return result, saved


def backward_block(grad_in, saved, pieces, params, sink):
    inward, outward, widen, narrow = params
    batch, length, width = grad_in.shape
    head = width // HEADS
    factor = head ** (-0.5)
    grad_out = grad_in.astype(f32)
    out = {}

    def weight(a, g):
        return jnp.einsum("bli,blj->ij", a, g, preferred_element_type=f32)

    feed_grad = (pieces[5][:, None] * grad_out).astype(bf16)
    if sink:
        feed_grad = sink("narrow", weight(saved["activated"], feed_grad), feed_grad)
    hidden_grad = (
        jnp.einsum("blj,ij->bli", feed_grad, narrow, preferred_element_type=f32)
        * saved["slope"].astype(f32)
    ).astype(bf16)
    if sink:
        hidden_grad = sink("widen", weight(saved["second_low"], hidden_grad), hidden_grad)
    second_grad = jnp.einsum("blj,ij->bli", hidden_grad, widen, preferred_element_type=f32)
    middle_grad = grad_out + normal_back(
        second_grad * (1.0 + pieces[4][:, None]), saved["m_norm"], saved["m_inverse"]
    )
    attention_grad = (pieces[2][:, None] * middle_grad).astype(bf16)
    if sink:
        attention_grad = sink("outward", weight(saved["attended"], attention_grad), attention_grad)
    attended_grad = jnp.einsum("blj,ij->bli", attention_grad, outward, preferred_element_type=f32)
    attended_grad = attended_grad.astype(bf16).reshape(batch, length, HEADS, head)
    view = saved["projected"].reshape(batch, length, 3, HEADS, head)
    value_grad = jnp.einsum(
        "bhlm,blhd->bmhd", saved["rounded"], attended_grad, preferred_element_type=f32
    )
    weight_grad = jnp.einsum(
        "blhd,bmhd->bhlm", attended_grad, view[:, :, 2], preferred_element_type=f32
    )
    soft = saved["soft"]
    score_grad = soft * (weight_grad - jnp.sum(weight_grad * soft, axis=-1, keepdims=True))
    score_grad = score_grad.astype(bf16)
    query_grad = (
        jnp.einsum("bhlm,bmhd->blhd", score_grad, view[:, :, 1], preferred_element_type=f32)
        * factor
    )
    key_grad = (
        jnp.einsum("bhlm,blhd->bmhd", score_grad, view[:, :, 0], preferred_element_type=f32)
        * factor
    )
    projected_grad = jnp.concatenate(
        [g.astype(bf16).reshape(batch, length, width) for g in (query_grad, key_grad, value_grad)],
        axis=-1,
    )
    if sink:
        projected_grad = sink("inward", weight(saved["first_low"], projected_grad), projected_grad)
    first_grad = jnp.einsum("blj,ij->bli", projected_grad, inward, preferred_element_type=f32)
    stream = middle_grad + normal_back(
        first_grad * (1.0 + pieces[1][:, None]), saved["x_norm"], saved["x_inverse"]
    )
    if sink:
        total = jnp.sum(projected_grad.astype(f32), axis=(0, 1))
        out["biases"] = jnp.concatenate(
            [
                total[:width],
                total[2 * width :],
                jnp.sum(attention_grad.astype(f32), axis=(0, 1)),
                jnp.sum(hidden_grad.astype(f32), axis=(0, 1)),
                jnp.sum(feed_grad.astype(f32), axis=(0, 1)),
            ]
        )
        out["modulated"] = jnp.concatenate(
            [
                jnp.sum(first_grad, axis=1),
                jnp.sum(first_grad * saved["x_norm"], axis=1),
                jnp.sum(middle_grad * saved["branch"], axis=1),
                jnp.sum(second_grad, axis=1),
                jnp.sum(second_grad * saved["m_norm"], axis=1),
                jnp.sum(grad_out * saved["feed"], axis=1),
            ],
            axis=-1,
        ).astype(bf16)
    return stream.astype(bf16), out


def pick(array, index):
    return lax.dynamic_index_in_dim(array, index, 0, keepdims=False)


def swap(array, bit, count):
    return lax.ppermute(array, "dp", [(i, i ^ (1 << bit)) for i in range(count)])


def turn(array, by, count):
    return lax.ppermute(array, "fsdp", [(i, (i + by) % count) for i in range(count)])


def assemble(place, shards, rounds, far, near):
    steps = len(rounds)
    share, columns = rounds[0].shape
    parts = far_parts = 4
    ways = steps + 1
    starts, begin = [], 0
    for shard in shards:
        starts.append(begin)
        begin += shard.shape[1]
    per_out = 1 + 4 * steps

    def kernel(place_ref, *refs):
        shard_refs = refs[: len(shards)]
        round_refs = refs[len(shards) : len(shards) + steps]
        far_refs = refs[len(shards) + steps : len(shards) + 2 * steps]
        near_ref = refs[len(shards) + 2 * steps]
        outs = refs[len(shards) + 2 * steps + 1 : -1]
        sems = refs[-1]
        f, d = place_ref[0], place_ref[1]
        core, side = lax.rem(d, 2), lax.div(d, 2)
        copies = []

        def add(source, target, rows, count):
            target_ref = target.at[pl.ds(pl.multiple_of(rows, 16), count)]
            copies.append(pltpu.make_async_copy(source, target_ref, sems.at[len(copies)]))

        for number, out in enumerate(outs):
            add(shard_refs[number], out, f * (parts * share), parts * share)
            cols = pl.ds(starts[number], shards[number].shape[1])
            for step in range(steps):
                owner = lax.rem(f + ways - 1 - step, ways)
                base = owner * (parts * share)
                same, other = side * 2 + core, (1 - side) * 2 + core
                add(round_refs[step].at[:, cols], out, base + same * share, share)
                add(far_refs[step].at[:, cols], out, base + other * share, share)
                same, other = side * 2 + 1 - core, (1 - side) * 2 + 1 - core
                add(near_ref.at[2 * step, :, cols], out, base + same * share, share)
                add(near_ref.at[2 * step + 1, :, cols], out, base + other * share, share)
        for copy in copies:
            copy.start()
        for copy in copies:
            copy.wait()

    any_space = pl.BlockSpec(memory_space=pl.ANY)
    return pl.pallas_call(
        kernel,
        out_shape=[
            jax.ShapeDtypeStruct((ways * parts * share, shard.shape[1]), bf16) for shard in shards
        ],
        in_specs=[pl.BlockSpec(memory_space=pltpu.SMEM)]
        + [any_space] * (len(shards) + 2 * steps + 1),
        out_specs=[any_space] * len(shards),
        scratch_shapes=[pltpu.SemaphoreType.DMA((per_out * len(shards),))],
    )(place, *shards, *rounds, *far, near)


def gather_weights(shards, fsdp, dp, f, d):
    share = shards[0].shape[0] // dp
    if dp != 4 or share % 16 or fsdp == 1:
        outs = []
        for shard in shards:
            own = lax.dynamic_slice_in_dim(shard, d * share, share, 0)
            outs.append(lax.all_gather(own, ("fsdp", "dp"), axis=0, tiled=True))
        return outs
    own = [lax.dynamic_slice_in_dim(shard, d * share, share, 0) for shard in shards]
    piece = jnp.concatenate(own, axis=1)
    rounds, far = [], []
    for step in range(1, fsdp):
        piece = turn(piece, 1, fsdp)
        rounds.append(piece)
        far.append(swap(piece, 1, dp))
    both = [member for pair in zip(rounds, far) for member in pair]
    near = swap(jnp.stack(both), 0, dp)
    return assemble(jnp.stack([f, d]), shards, rounds, far, near)


def gather_small(array, fsdp, dp):
    whole = jnp.stack([array] + [turn(array, step, fsdp) for step in range(1, fsdp)])[:, None]
    return spread_small(whole, dp)


def spread_small(whole, dp):
    for bit in reversed(range(dp.bit_length() - 1)):
        whole = jnp.stack([whole, swap(whole, bit, dp)], axis=2)
        whole = whole.reshape((whole.shape[0], -1) + whole.shape[3:])
    return whole


def reduce_weights(grads, fsdp, dp, d, f):
    bits = dp.bit_length() - 1
    helds = []
    for grad in grads:
        rows, columns = grad.shape
        share = rows // (fsdp * dp)
        helds.append(grad.astype(bf16).reshape((fsdp,) + (2,) * bits + (share, columns)))
    held, first = None, True
    for bit in range(bits):
        mine = (d >> bit) & 1
        axis = bits - bit

        def part(which):
            if first:
                return jnp.concatenate(
                    [lax.dynamic_index_in_dim(h, which, axis, keepdims=False) for h in helds], -1
                )
            return lax.dynamic_index_in_dim(held, which, axis, keepdims=False)

        got = swap(part(1 - mine), bit, dp)
        held, first = (part(mine).astype(f32) + got.astype(f32)).astype(bf16), False
    total = pick(held, f).astype(f32)
    for step in range(1, fsdp):
        total += turn(pick(held, lax.rem(f + step, fsdp)), step, fsdp).astype(f32)
    whole = total.astype(bf16)[None]
    for bit in reversed(range(bits)):
        mine = (d >> bit) & 1
        got = swap(whole, bit, dp)
        low = jnp.where(mine == 0, whole, got)
        high = jnp.where(mine == 0, got, whole)
        whole = jnp.stack([low, high], axis=1).reshape((-1,) + whole.shape[1:])
    whole = whole.reshape((-1, whole.shape[-1])).astype(f32)
    shares, begin = [], 0
    for grad in grads:
        shares.append(whole[:, begin : begin + grad.shape[1]])
        begin += grad.shape[1]
    return shares


def per_device(
    latents, cotangent, timesteps, classes,
    modulation, inward, outward, widen, narrow, biases, class_table,
):
    section_zero = lax.axis_index("section") == 0
    fsdp, dp = lax.axis_size("fsdp"), lax.axis_size("dp")
    f, d = lax.axis_index("fsdp"), lax.axis_index("dp")
    batch, length, width = latents.shape
    table_rows = class_table.shape[0]
    slice_width = modulation.shape[1]
    bias_share = biases.shape[1]
    hidden_units = widen.shape[2]
    everyone = fsdp * dp * batch

    inward_all, outward_all = gather_weights([inward[0], outward[0]], fsdp, dp, f, d)
    (widen_all,) = gather_weights([widen[0]], fsdp, dp, f, d)
    (narrow_all,) = gather_weights([narrow[0]], fsdp, dp, f, d)
    params = (inward_all, outward_all, widen_all, narrow_all)

    own = jnp.concatenate([timesteps.astype(f32), classes.astype(f32), biases[0].astype(f32)])
    line = jnp.stack([own] + [turn(own, step, fsdp) for step in range(1, fsdp)])
    back = lax.rem(f + fsdp - jnp.arange(fsdp), fsdp)
    every_bias = line[:, 2 * batch :][back].reshape(-1)
    ids = spread_small(line[:, None, : 2 * batch], dp)
    steps = ids[..., :batch].reshape(-1)
    labels = f * table_rows + jnp.arange(table_rows, dtype=jnp.int32)
    onehot = (
        ids[..., batch:].reshape(-1).astype(jnp.int32)[:, None] == labels[None, :]
    ).astype(bf16)
    found = dot(onehot, class_table, ((1,), (0,))).astype(bf16)
    found = found.reshape(fsdp, dp * batch, width)

    def columns(index):
        return lax.dynamic_slice_in_dim(found, index * slice_width, slice_width, 2)

    rows = columns(f).astype(f32)
    for step in range(1, fsdp):
        sent = jnp.roll(columns(lax.rem(f + step, fsdp)), step, axis=0)
        rows += turn(sent, step, fsdp).astype(f32)
    features = lax.dynamic_slice_in_dim(
        timestep_features(steps, width), f * slice_width, slice_width, 1
    )
    condition = features + rows.reshape(everyone, slice_width)
    low_slice = jax.nn.silu(condition).astype(bf16)
    group = low_slice.reshape(fsdp, dp, batch, slice_width)[:, 0]
    partial = dot(group.reshape(fsdp * batch, slice_width), modulation[0], ((1,), (0,)))
    partial = partial.reshape(fsdp, batch, -1)
    modulated = partial[0] + every_bias[: 6 * width]
    for step in range(1, fsdp):
        modulated += turn(partial[step], -step, fsdp)
    pieces = jnp.split(modulated, 6, axis=-1)
    bias = {
        "in": jnp.concatenate(
            [
                every_bias[6 * width : 7 * width],
                jnp.zeros((width,), f32),
                every_bias[7 * width : 8 * width],
            ]
        ),
        "out": every_bias[8 * width : 9 * width],
        "ff1": every_bias[9 * width : 9 * width + hidden_units],
        "ff2": every_bias[9 * width + hidden_units :],
    }

    first, unused = forward_block(latents, pieces, params, bias)
    incoming = lax.ppermute(first, "section", [(0, 1)])
    block_in = jnp.where(section_zero, latents, incoming)
    section_output, saved = forward_block(block_in, pieces, params, bias)
    early, unused = backward_block(cotangent, saved, pieces, params, None)
    returning = lax.ppermute(early, "section", [(1, 0)])
    grad_in = jnp.where(section_zero, returning, cotangent)
    made = {}

    def sink(name, grad, after):
        made[name], after = lax.optimization_barrier((grad.astype(bf16), after))
        return after

    input_gradient, grads = backward_block(grad_in, saved, pieces, params, sink)
    (narrow_share,) = reduce_weights([made["narrow"]], fsdp, dp, d, f)
    (widen_share,) = reduce_weights([made["widen"]], fsdp, dp, d, f)
    inward_share, outward_share = reduce_weights([made["inward"], made["outward"]], fsdp, dp, d, f)

    tail = jnp.concatenate([grads["modulated"].reshape(-1), grads["biases"].astype(bf16)])
    tail = gather_small(tail.reshape(-1, width), fsdp, dp).reshape(fsdp * dp, -1)
    count = batch * 6 * width
    modulated_grad = tail[:, :count].reshape(everyone, 6 * width)
    bias_grad = jnp.concatenate(
        [
            jnp.sum(modulated_grad.astype(f32), axis=0),
            jnp.sum(tail[:, count:].astype(f32), axis=0),
        ]
    )
    bias_grad = lax.dynamic_slice_in_dim(bias_grad, f * bias_share, bias_share, 0)
    modulation_grad = dot(low_slice, modulated_grad, ((0,), (0,)))
    condition_grad = dot(modulated_grad, modulation[0], ((1,), (1,)))
    count = lax.axis_size("section")
    for step in range(1, count):
        condition_grad += lax.ppermute(
            condition_grad, "section", [(i, (i + step) % count) for i in range(count)]
        )
    gate = jax.nn.sigmoid(condition)
    condition_grad = condition_grad * (gate * (1.0 + condition * (1.0 - gate)))
    condition_grad = condition_grad.reshape(fsdp, dp * batch, slice_width)
    gathered = [condition_grad]
    for step in range(1, fsdp):
        sent = jnp.roll(condition_grad, step, axis=0)
        gathered.append(turn(sent, step, fsdp))
    gathered = jnp.stack(gathered)[back]
    gathered = jnp.moveaxis(gathered, 0, 2).reshape(everyone, width)
    table_grad = lax.dot_general(
        onehot.astype(f32), gathered, (((0,), (0,)), ((), ())), precision=lax.Precision.HIGHEST
    )
    return (
        section_output[None],
        input_gradient[None],
        modulation_grad[None],
        inward_share[None],
        outward_share[None],
        widen_share[None],
        narrow_share[None],
        bias_grad[None],
        table_grad,
    )


def solution(mesh):
    return jax.shard_map(
        per_device,
        mesh=mesh,
        in_specs=(
            P(("fsdp", "dp"), None, None),
            P(("fsdp", "dp"), None, None),
            P(("fsdp", "dp")),
            P(("fsdp", "dp")),
            P("section", "fsdp", None),
            P("section", "fsdp", None),
            P("section", "fsdp", None),
            P("section", "fsdp", None),
            P("section", "fsdp", None),
            P("section", "fsdp"),
            P("fsdp", None),
        ),
        out_specs=(
            P("section", ("fsdp", "dp"), None, None),
            P("section", ("fsdp", "dp"), None, None),
            P("section", "fsdp", None),
            P("section", "fsdp", None),
            P("section", "fsdp", None),
            P("section", "fsdp", None),
            P("section", "fsdp", None),
            P("section", "fsdp"),
            P("fsdp", None),
        ),
        check_vma=False,
    )
```

```python
import math

import jax
import jax.numpy as jnp
from jax import lax
from jax.experimental import pallas as pl
from jax.experimental.pallas import tpu as pltpu
from jax.sharding import PartitionSpec as P

HEADS = 12

eps = 1e-06
f32 = jnp.float32
bf16 = jnp.bfloat16


def dot(left, right, dims):
    return lax.dot_general(left, right, (dims, ((), ())), preferred_element_type=f32)


def normalize(values):
    average = jnp.mean(values, axis=-1, keepdims=True)
    centred = values - average
    variance = jnp.mean(centred * centred, axis=-1, keepdims=True)
    inverse = lax.rsqrt(variance + eps)
    return (centred * inverse, inverse)


def normal_back(grad_normed, normed, inverse):
    first_mean = jnp.mean(grad_normed, axis=-1, keepdims=True)
    cross_mean = jnp.mean(grad_normed * normed, axis=-1, keepdims=True)
    return inverse * (grad_normed - first_mean - normed * cross_mean)


def timestep_features(step_ids, model_width):
    half_width = model_width // 2
    frequencies = jnp.exp(
        -math.log(10000.0) * jnp.arange(half_width, dtype=f32) / half_width
    )
    angles = step_ids[:, None] * frequencies[None, :]
    return jnp.concatenate([jnp.cos(angles), jnp.sin(angles)], axis=-1)


def gelu_and_slope(hidden):
    c = math.sqrt(2.0 / math.pi)
    squared = hidden * hidden
    t = jnp.tanh(c * hidden * (1.0 + 0.044715 * squared))
    value = 0.5 * hidden * (1.0 + t)
    slope = 0.5 * (1.0 + t) + 0.5 * hidden * (1.0 - t * t) * c * (1.0 + 3 * 0.044715 * squared)
    return value, slope


PAIR = 2


def pair_columns(ref, part, pair, lanes, width):
    return ref[0, :, part * width + pair * lanes : part * width + (pair + 1) * lanes]


def soft_rows(query, key, factor):
    scores = dot(query, key, ((1,), (1,))) * factor
    raised = jnp.exp(scores - jnp.max(scores, axis=-1, keepdims=True))
    return raised / jnp.sum(raised, axis=-1, keepdims=True)


def attention(projected):
    batch, length, width = projected.shape[0], projected.shape[1], projected.shape[2] // 3
    head = width // HEADS
    lanes = PAIR * head

    def kernel(in_ref, out_ref):
        owner = lax.broadcasted_iota(jnp.int32, (length, lanes), 1) // head
        for pair in range(HEADS // PAIR):
            q, k, v = (pair_columns(in_ref, part, pair, lanes, width) for part in range(3))
            out = jnp.zeros((length, lanes), f32)
            for i in range(PAIR):
                soft = soft_rows(jnp.where(owner == i, q, 0), k, head ** (-0.5))
                out = jnp.where(owner == i, dot(soft.astype(bf16), v, ((1,), (0,))), out)
            out_ref[0, :, pair * lanes : (pair + 1) * lanes] = out.astype(bf16)

    return pl.pallas_call(
        kernel,
        grid=(batch,),
        in_specs=[pl.BlockSpec((1, length, 3 * width), lambda b: (b, 0, 0))],
        out_specs=pl.BlockSpec((1, length, width), lambda b: (b, 0, 0)),
        out_shape=jax.ShapeDtypeStruct((batch, length, width), bf16),
        compiler_params=pltpu.CompilerParams(vmem_limit_bytes=40 * 1024 * 1024),
        cost_estimate=pl.CostEstimate(
            flops=4 * batch * length * length * width,
            bytes_accessed=8 * batch * length * width,
            transcendentals=batch * HEADS * length * length,
        ),
    )(projected)


def attention_back(projected, grad):
    batch, length, width = grad.shape
    head = width // HEADS
    lanes = PAIR * head
    factor = head ** (-0.5)

    def kernel(in_ref, grad_ref, out_ref):
        owner = lax.broadcasted_iota(jnp.int32, (length, lanes), 1) // head
        for pair in range(HEADS // PAIR):
            q, k, v = (pair_columns(in_ref, part, pair, lanes, width) for part in range(3))
            g = pair_columns(grad_ref, 0, pair, lanes, width)
            outs = [jnp.zeros((length, lanes), f32)] * 3
            for i in range(PAIR):
                soft = soft_rows(jnp.where(owner == i, q, 0), k, factor)
                weight = dot(jnp.where(owner == i, g, 0), v, ((1,), (1,)))
                centre = jnp.sum(weight * soft, axis=-1, keepdims=True)
                score = (soft * (weight - centre)).astype(bf16)
                made = (
                    dot(score, k, ((1,), (0,))) * factor,
                    dot(score, q, ((0,), (0,))) * factor,
                    dot(soft.astype(bf16), g, ((0,), (0,))),
                )
                outs = [jnp.where(owner == i, new, old) for new, old in zip(made, outs)]
            for part in range(3):
                begin = part * width + pair * lanes
                out_ref[0, :, begin : begin + lanes] = outs[part].astype(bf16)

    return pl.pallas_call(
        kernel,
        grid=(batch,),
        in_specs=[
            pl.BlockSpec((1, length, 3 * width), lambda b: (b, 0, 0)),
            pl.BlockSpec((1, length, width), lambda b: (b, 0, 0)),
        ],
        out_specs=pl.BlockSpec((1, length, 3 * width), lambda b: (b, 0, 0)),
        out_shape=jax.ShapeDtypeStruct((batch, length, 3 * width), bf16),
        compiler_params=pltpu.CompilerParams(vmem_limit_bytes=40 * 1024 * 1024),
        cost_estimate=pl.CostEstimate(
            flops=10 * batch * length * length * width,
            bytes_accessed=14 * batch * length * width,
            transcendentals=batch * HEADS * length * length,
        ),
    )(projected, grad)


def feed_forward(low, widen, first_bias, narrow):
    batch, length, width = low.shape
    rows, units = batch * length, widen.shape[1]
    tile = 512

    def kernel(low_ref, widen_ref, bias_ref, narrow_ref, active_ref, slope_ref, feed_ref):
        hidden = dot(low_ref[...], widen_ref[...], ((1,), (0,))) + bias_ref[...]
        value, slope = gelu_and_slope(hidden)
        active = value.astype(bf16)
        active_ref[...] = active
        slope_ref[...] = slope.astype(bf16)
        part = dot(active, narrow_ref[...], ((1,), (0,)))

        @pl.when(pl.program_id(0) == 0)
        def _():
            feed_ref[...] = part

        @pl.when(pl.program_id(0) > 0)
        def _():
            feed_ref[...] += part

    active, slope, feed = pl.pallas_call(
        kernel,
        grid=(units // tile,),
        in_specs=[
            pl.BlockSpec((rows, width), lambda j: (0, 0)),
            pl.BlockSpec((width, tile), lambda j: (0, j)),
            pl.BlockSpec((1, tile), lambda j: (0, j)),
            pl.BlockSpec((tile, width), lambda j: (j, 0)),
        ],
        out_specs=[
            pl.BlockSpec((rows, tile), lambda j: (0, j)),
            pl.BlockSpec((rows, tile), lambda j: (0, j)),
            pl.BlockSpec((rows, width), lambda j: (0, 0)),
        ],
        out_shape=[
            jax.ShapeDtypeStruct((rows, units), bf16),
            jax.ShapeDtypeStruct((rows, units), bf16),
            jax.ShapeDtypeStruct((rows, width), f32),
        ],
        compiler_params=pltpu.CompilerParams(vmem_limit_bytes=48 * 1024 * 1024),
        cost_estimate=pl.CostEstimate(
            flops=4 * rows * width * units,
            bytes_accessed=4 * width * units + 4 * rows * units + 6 * rows * width,
            transcendentals=rows * units,
        ),
    )(low.reshape(rows, width), widen, first_bias[None], narrow)
    return (
        active.reshape(batch, length, units),
        slope.reshape(batch, length, units),
        feed.reshape(batch, length, width),
    )


def pack_pieces(widen_rows, narrow_rows):
    count, share, units = widen_rows.shape
    width = narrow_rows.shape[-1]
    beside = narrow_rows.reshape(count, units // width, share, width)
    beside = jnp.swapaxes(beside, 1, 2).reshape(count, share, units)
    return jnp.concatenate([widen_rows, beside], axis=1)


def unpack_pieces(packed, width):
    count, double, units = packed.shape
    share = double // 2
    narrow_rows = packed[:, share:].reshape(count, share, units // width, width)
    narrow_rows = jnp.swapaxes(narrow_rows, 1, 2).reshape(-1, width)
    return packed[:, :share].reshape(-1, units), narrow_rows


def first_feed_forward(low, packed, first_bias, ways):
    batch, length, width = low.shape
    count, double, units = packed.shape
    rows, share, tile, group = batch * length, double // 2, units // ways, count // ways
    side = units // width

    def kernel(low_ref, widen_ref, narrow_ref, bias_ref, widen_out, narrow_out, feed_ref):
        widen = widen_ref[...].reshape(width, tile)
        parts = [narrow_ref[:, :, r * width : (r + 1) * width] for r in range(side)]
        narrow = jnp.stack(parts, axis=1).reshape(tile, width)
        widen_out[...] = widen
        narrow_out[...] = narrow
        hidden = dot(low_ref[...], widen, ((1,), (0,))) + bias_ref[...]
        active = gelu_and_slope(hidden)[0].astype(bf16)
        part = dot(active, narrow, ((1,), (0,)))

        @pl.when(pl.program_id(0) == 0)
        def _():
            feed_ref[...] = part

        @pl.when(pl.program_id(0) > 0)
        def _():
            feed_ref[...] += part

    widen, narrow, feed = pl.pallas_call(
        kernel,
        grid=(ways,),
        in_specs=[
            pl.BlockSpec((rows, width), lambda j: (0, 0)),
            pl.BlockSpec((count, share, tile), lambda j: (0, 0, j)),
            pl.BlockSpec((group, share, units), lambda j: (j, 1, 0)),
            pl.BlockSpec((1, tile), lambda j: (0, j)),
        ],
        out_specs=[
            pl.BlockSpec((width, tile), lambda j: (0, j)),
            pl.BlockSpec((tile, width), lambda j: (j, 0)),
            pl.BlockSpec((rows, width), lambda j: (0, 0)),
        ],
        out_shape=[
            jax.ShapeDtypeStruct((width, units), bf16),
            jax.ShapeDtypeStruct((units, width), bf16),
            jax.ShapeDtypeStruct((rows, width), f32),
        ],
        compiler_params=pltpu.CompilerParams(vmem_limit_bytes=48 * 1024 * 1024),
        cost_estimate=pl.CostEstimate(
            flops=4 * rows * width * units,
            bytes_accessed=8 * width * units + 6 * rows * width,
            transcendentals=rows * units,
        ),
    )(low.reshape(rows, width), packed, packed, first_bias[None])
    return widen, narrow, feed.reshape(batch, length, width)


def feed_weight_grads(low, hidden_grad, active, feed_grad, ways, count):
    width, units = low.shape[-1], active.shape[-1]
    rows = low.shape[0] * low.shape[1]
    share, group, tile, side = width // count, count // ways, units // ways, units // width

    def kernel(low_ref, hidden_ref, active_ref, feed_ref, out_ref):
        widen = dot(low_ref[...], hidden_ref[...], ((1,), (0,))).astype(bf16)
        out_ref[:, :share, :] = widen.reshape(group, share, units)
        narrow = dot(active_ref[...], feed_ref[...], ((0,), (0,))).astype(bf16)
        narrow = narrow.reshape(group, side, share, width)
        for r in range(side):
            out_ref[:, share:, r * width : (r + 1) * width] = narrow[:, r]

    return pl.pallas_call(
        kernel,
        grid=(ways,),
        in_specs=[
            pl.BlockSpec((width // ways, rows), lambda j: (j, 0)),
            pl.BlockSpec((rows, units), lambda j: (0, 0)),
            pl.BlockSpec((rows, tile), lambda j: (0, j)),
            pl.BlockSpec((rows, width), lambda j: (0, 0)),
        ],
        out_specs=pl.BlockSpec((group, 2 * share, units), lambda j: (j, 0, 0)),
        out_shape=jax.ShapeDtypeStruct((count, 2 * share, units), bf16),
        compiler_params=pltpu.CompilerParams(vmem_limit_bytes=48 * 1024 * 1024),
        cost_estimate=pl.CostEstimate(
            flops=4 * rows * width * units,
            bytes_accessed=4 * width * units + 4 * rows * (width + units),
            transcendentals=0,
        ),
    )(
        low.reshape(rows, width).T,
        hidden_grad.reshape(rows, units),
        active.reshape(rows, units),
        feed_grad.reshape(rows, width),
    )


def unpack_shares(place, pieces, width):
    count = len(pieces)
    double, units = pieces[0].shape
    share, side = double // 2, units // width

    def kernel(place_ref, *refs):
        widen_ref, narrow_ref = refs[count:]
        for number in range(count):
            at = place_ref[number]
            rows = pl.ds(pl.multiple_of(at * share, 8), share)
            widen_ref[rows, :] = refs[number][:share, :].astype(f32)
            for r in range(side):
                rows = pl.ds(pl.multiple_of((at * side + r) * share, 8), share)
                part = refs[number][share:, r * width : (r + 1) * width]
                narrow_ref[rows, :] = part.astype(f32)

    whole = pl.BlockSpec(memory_space=pltpu.VMEM)
    return pl.pallas_call(
        kernel,
        in_specs=[pl.BlockSpec(memory_space=pltpu.SMEM)] + [whole] * count,
        out_specs=[whole, whole],
        out_shape=[
            jax.ShapeDtypeStruct((count * share, units), f32),
            jax.ShapeDtypeStruct((count * side * share, width), f32),
        ],
        compiler_params=pltpu.CompilerParams(vmem_limit_bytes=40 * 1024 * 1024),
    )(place, *pieces)


def forward_block(x_in, pieces, params, bias, run_feed=None):
    inward, outward, widen, narrow = params
    batch, length, width = x_in.shape
    x = x_in.astype(f32)
    first_norm, first_inverse = normalize(x)
    first_low = (first_norm * (1.0 + pieces[1][:, None]) + pieces[0][:, None]).astype(bf16)
    projected = (
        jnp.einsum("bli,ij->blj", first_low, inward, preferred_element_type=f32) + bias["in"]
    ).astype(bf16)
    attended = attention(projected)
    branch = jnp.einsum("bli,ij->blj", attended, outward, preferred_element_type=f32) + bias["out"]
    middle = x + pieces[2][:, None] * branch
    second_norm, second_inverse = normalize(middle)
    second_low = (second_norm * (1.0 + pieces[4][:, None]) + pieces[3][:, None]).astype(bf16)
    if run_feed:
        return middle + pieces[5][:, None] * (run_feed(second_low) + bias["ff2"])
    activated, slope, feed = feed_forward(second_low, widen, bias["ff1"], narrow)
    feed = feed + bias["ff2"]
    result = (middle + pieces[5][:, None] * feed).astype(bf16)
    saved = dict(
        x_norm=first_norm, x_inverse=first_inverse, first_low=first_low, projected=projected,
        attended=attended, branch=branch, m_norm=second_norm,
        m_inverse=second_inverse, second_low=second_low, slope=slope,
        activated=activated, feed=feed,
    )
    return result, saved


def backward_block(grad_in, saved, pieces, params, sink, hook):
    inward, outward, widen, narrow = params
    batch, length, width = grad_in.shape
    grad_out = grad_in.astype(f32)
    out = {}

    def weight(a, g):
        return jnp.einsum("bli,blj->ij", a, g, preferred_element_type=f32)

    feed_grad = (pieces[5][:, None] * grad_out).astype(bf16)
    hidden_grad = (
        jnp.einsum("blj,ij->bli", feed_grad, narrow, preferred_element_type=f32)
        * saved["slope"].astype(f32)
    ).astype(bf16)
    if sink:
        operands = (saved["second_low"], hidden_grad, saved["activated"], feed_grad)
        hidden_grad = sink("feed", operands, hidden_grad)
    second_grad = jnp.einsum("blj,ij->bli", hidden_grad, widen, preferred_element_type=f32)
    middle_grad = grad_out + normal_back(
        second_grad * (1.0 + pieces[4][:, None]), saved["m_norm"], saved["m_inverse"]
    )
    attention_grad = (pieces[2][:, None] * middle_grad).astype(bf16)
    if sink:
        attention_grad = sink("outward", weight(saved["attended"], attention_grad), attention_grad)
    attended_grad = jnp.einsum("blj,ij->bli", attention_grad, outward, preferred_element_type=f32)
    attended_grad = hook("attended", attended_grad.astype(bf16))
    projected_grad = attention_back(saved["projected"], attended_grad)
    if sink:
        projected_grad = sink("inward", weight(saved["first_low"], projected_grad), projected_grad)
    first_grad = jnp.einsum("blj,ij->bli", projected_grad, inward, preferred_element_type=f32)
    first_grad = hook("first", first_grad)
    stream = middle_grad + normal_back(
        first_grad * (1.0 + pieces[1][:, None]), saved["x_norm"], saved["x_inverse"]
    )
    if sink:
        total = jnp.sum(projected_grad.astype(f32), axis=(0, 1))
        out["biases"] = jnp.concatenate(
            [
                total[:width],
                total[2 * width :],
                jnp.sum(attention_grad.astype(f32), axis=(0, 1)),
                jnp.sum(hidden_grad.astype(f32), axis=(0, 1)),
                jnp.sum(feed_grad.astype(f32), axis=(0, 1)),
            ]
        )
        out["modulated"] = jnp.concatenate(
            [
                jnp.sum(first_grad, axis=1),
                jnp.sum(first_grad * saved["x_norm"], axis=1),
                jnp.sum(middle_grad * saved["branch"], axis=1),
                jnp.sum(second_grad, axis=1),
                jnp.sum(second_grad * saved["m_norm"], axis=1),
                jnp.sum(grad_out * saved["feed"], axis=1),
            ],
            axis=-1,
        ).astype(bf16)
    return stream.astype(bf16), out


def pick(array, index):
    return lax.dynamic_index_in_dim(array, index, 0, keepdims=False)


def swap(array, bit, count):
    return lax.ppermute(array, "dp", [(i, i ^ (1 << bit)) for i in range(count)])


def turn(array, by, count):
    return lax.ppermute(array, "fsdp", [(i, (i + by) % count) for i in range(count)])


def assemble(place, shards, rounds, far, near, near_far):
    steps = len(rounds)
    share, columns = rounds[0].shape
    parts = far_parts = 4
    ways = steps + 1
    starts, begin = [], 0
    for shard in shards:
        starts.append(begin)
        begin += shard.shape[1]

    def kernel(place_ref, *refs):
        shard_refs = refs[: len(shards)]
        round_refs = refs[len(shards) : len(shards) + steps]
        far_refs = refs[len(shards) + steps : len(shards) + 2 * steps]
        near_refs = refs[len(shards) + 2 * steps : len(shards) + 3 * steps]
        near_far_refs = refs[len(shards) + 3 * steps : len(shards) + 4 * steps]
        outs = refs[len(shards) + 4 * steps :]
        f, d = place_ref[0], place_ref[1]
        core, side = lax.rem(d, 2), lax.div(d, 2)

        def put(out, rows, value):
            out[pl.ds(pl.multiple_of(rows, 16), value.shape[0]), :] = value

        for number, out in enumerate(outs):
            for part in range(parts):
                put(
                    out,
                    (f * parts + part) * share,
                    shard_refs[number][part * share : (part + 1) * share, :],
                )
            begin, end = starts[number], starts[number] + shards[number].shape[1]
            for step in range(steps):
                owner = lax.rem(f + ways - 1 - step, ways)
                base = owner * (parts * share)
                same, other = side * 2 + core, (1 - side) * 2 + core
                put(out, base + same * share, round_refs[step][:, begin:end])
                put(out, base + other * share, far_refs[step][:, begin:end])
                same, other = side * 2 + 1 - core, (1 - side) * 2 + 1 - core
                put(out, base + same * share, near_refs[step][:, begin:end])
                put(out, base + other * share, near_far_refs[step][:, begin:end])

    whole = pl.BlockSpec(memory_space=pltpu.VMEM)
    return pl.pallas_call(
        kernel,
        out_shape=[
            jax.ShapeDtypeStruct((ways * parts * share, shard.shape[1]), bf16) for shard in shards
        ],
        in_specs=[pl.BlockSpec(memory_space=pltpu.SMEM)] + [whole] * (len(shards) + 4 * steps),
        out_specs=[whole] * len(shards),
        compiler_params=pltpu.CompilerParams(vmem_limit_bytes=40 * 1024 * 1024),
    )(place, *shards, *rounds, *far, *near, *near_far)


def tie(value, *others):
    return lax.optimization_barrier((value,) + others)[0]


class Gather:
    def __init__(self, shards, fsdp, dp, f, d):
        self.shards, self.sizes, self.place = shards, (fsdp, dp), (f, d)
        share = shards[0].shape[0] // dp
        own = [lax.dynamic_slice_in_dim(shard, d * share, share, 0) for shard in shards]
        self.plain = dp != 4 or share % 16 != 0 or fsdp == 1
        if self.plain:
            self.outs = [lax.all_gather(o, ("fsdp", "dp"), axis=0, tiled=True) for o in own]
        else:
            self.own = jnp.concatenate(own, axis=1)
            self.rounds, self.far, self.near, self.near_far = [], [], [], []

    def begin(self):
        if not self.plain:
            self.rounds.append(turn(self.own, 1, self.sizes[0]))

    def forward(self):
        if self.plain:
            return self.outs[0]
        fsdp, dp = self.sizes
        last = self.rounds[-1]
        if len(self.rounds) < fsdp - 1:
            self.rounds.append(turn(last, 1, fsdp))
        self.far.append(swap(last, 1, dp))
        self.near.append(swap(last, 0, dp))
        self.near_far.append(swap(self.far[-1], 0, dp))
        return last

    def finish(self):
        if self.plain:
            return self.outs
        while len(self.far) < len(self.rounds):
            self.forward()
        return assemble(
            jnp.stack(self.place), self.shards, self.rounds, self.far, self.near, self.near_far
        )


def gather_small(array, fsdp, dp):
    whole = jnp.stack([array] + [turn(array, step, fsdp) for step in range(1, fsdp)])[:, None]
    return spread_small(whole, dp)


def spread_small(whole, dp):
    for bit in reversed(range(dp.bit_length() - 1)):
        whole = jnp.stack([whole, swap(whole, bit, dp)], axis=2)
        whole = whole.reshape((whole.shape[0], -1) + whole.shape[3:])
    return whole


class Reduce:
    def __init__(self, grads, fsdp, dp, f, d):
        self.sizes, self.place = (fsdp, dp), (f, d)
        self.bits = dp.bit_length() - 1
        self.widths = [grad.shape[1] for grad in grads]
        self.helds = []
        for grad in grads:
            share = grad.shape[0] // (fsdp * dp)
            shape = (fsdp,) + (2,) * self.bits + (share, grad.shape[1])
            self.helds.append(grad.astype(bf16).reshape(shape))
        self.bit = 0
        self.send()

    def part(self, which):
        axis = self.bits - self.bit
        parts = [lax.dynamic_index_in_dim(h, which, axis, keepdims=False) for h in self.helds]
        return jnp.concatenate(parts, -1) if len(parts) > 1 else parts[0]

    def send(self):
        mine = (self.place[1] >> self.bit) & 1
        self.kept = self.part(mine)
        self.got = swap(self.part(1 - mine), self.bit, self.sizes[1])

    def halve(self):
        got = self.got
        held = (self.kept.astype(f32) + got.astype(f32)).astype(bf16)
        self.helds = [held]
        self.bit += 1
        if self.bit < self.bits:
            self.send()
            return got
        fsdp, f = self.sizes[0], self.place[0]
        self.total = [pick(held, f).astype(f32)]
        for step in range(1, fsdp):
            self.total.append(turn(pick(held, lax.rem(f + step, fsdp)), step, fsdp).astype(f32))
        return got

    def finish(self):
        d, dp = self.place[1], self.sizes[1]
        whole = sum(self.total).astype(bf16)[None]
        for bit in reversed(range(self.bits)):
            mine = (d >> bit) & 1
            got = swap(whole, bit, dp)
            low = jnp.where(mine == 0, whole, got)
            high = jnp.where(mine == 0, got, whole)
            whole = jnp.stack([low, high], axis=1).reshape((-1,) + whole.shape[1:])
        whole = whole.reshape((-1, whole.shape[-1])).astype(f32)
        shares, begin = [], 0
        for width in self.widths:
            shares.append(whole[:, begin : begin + width])
            begin += width
        return shares


def per_device(
    latents, cotangent, timesteps, classes,
    modulation, inward, outward, widen, narrow, biases, class_table,
):
    section_zero = lax.axis_index("section") == 0
    fsdp, dp = lax.axis_size("fsdp"), lax.axis_size("dp")
    f, d = lax.axis_index("fsdp"), lax.axis_index("dp")
    batch, length, width = latents.shape
    table_rows = class_table.shape[0]
    slice_width = modulation.shape[1]
    bias_share = biases.shape[1]
    hidden_units = widen.shape[2]
    everyone = fsdp * dp * batch

    def own_piece(shard):
        rows = shard.shape[1] // dp
        return lax.dynamic_slice_in_dim(shard[0], d * rows, rows, 0)

    whole_tiles = dp == 4 and widen.shape[1] % (16 * dp) == 0
    packed = pack_pieces(own_piece(widen)[None], own_piece(narrow)[None])[0]
    packed = lax.all_gather(packed, ("fsdp", "dp"), axis=0)
    chunk = Gather([inward[0], outward[0]], fsdp, dp, f, d)

    own = jnp.concatenate([timesteps.astype(f32), classes.astype(f32), biases[0].astype(f32)])
    if not chunk.plain:
        own = tie(own, chunk.own)
    chunk.begin()
    line = jnp.stack([own] + [turn(own, step, fsdp) for step in range(1, fsdp)])
    line = tie(line, chunk.forward())
    back = lax.rem(f + fsdp - jnp.arange(fsdp), fsdp)
    every_bias = line[:, 2 * batch :][back].reshape(-1)
    labels = f * table_rows + jnp.arange(table_rows, dtype=jnp.int32)

    def onehot_of(ids):
        return (ids.reshape(-1).astype(jnp.int32)[:, None] == labels[None, :]).astype(bf16)

    found = dot(onehot_of(line[:, batch : 2 * batch]), class_table, ((1,), (0,))).astype(bf16)
    found = found.reshape(fsdp, batch, width)

    def columns(index):
        return lax.dynamic_slice_in_dim(found, index * slice_width, slice_width, 2)

    rows = columns(f).astype(f32)
    for step in range(1, fsdp):
        sent = jnp.roll(columns(lax.rem(f + step, fsdp)), step, axis=0)
        rows += turn(sent, step, fsdp).astype(f32)
    features = lax.dynamic_slice_in_dim(
        timestep_features(line[:, :batch].reshape(-1), width), f * slice_width, slice_width, 1
    )
    condition = features.reshape(fsdp, batch, slice_width) + rows
    group = jax.nn.silu(condition).astype(bf16).reshape(fsdp * batch, slice_width)
    group = tie(group, chunk.forward())
    partial = dot(group, modulation[0], ((1,), (0,)))
    partial = tie(partial, chunk.forward())
    partial = partial.reshape(fsdp, batch, -1)
    modulated = partial[0] + every_bias[: 6 * width]
    for step in range(1, fsdp):
        modulated += turn(partial[step], -step, fsdp)
    inward_all, outward_all = chunk.finish()
    params = (inward_all, outward_all, None, None)
    pieces = jnp.split(modulated, 6, axis=-1)
    bias = {
        "in": jnp.concatenate(
            [
                every_bias[6 * width : 7 * width],
                jnp.zeros((width,), f32),
                every_bias[7 * width : 8 * width],
            ]
        ),
        "out": every_bias[8 * width : 9 * width],
        "ff1": every_bias[9 * width : 9 * width + hidden_units],
        "ff2": every_bias[9 * width + hidden_units :],
    }

    weights = []

    def run_feed(low):
        if whole_tiles:
            widen_all, narrow_all, feed = first_feed_forward(low, packed, bias["ff1"], fsdp)
        else:
            widen_all, narrow_all = unpack_pieces(packed, width)
            feed = feed_forward(low, widen_all, bias["ff1"], narrow_all)[2]
        weights.extend([widen_all, narrow_all])
        return feed

    first = forward_block(latents, pieces, params, bias, run_feed).astype(bf16)
    params = (inward_all, outward_all, *weights)
    incoming = lax.ppermute(first, "section", [(0, 1)])
    ids = spread_small(line[:, None, batch : 2 * batch], dp)
    condition = spread_small(condition[:, None], dp).reshape(everyone, slice_width)
    incoming, condition, ids = lax.optimization_barrier((incoming, condition, ids))
    low_slice = jax.nn.silu(condition).astype(bf16)
    onehot = onehot_of(ids)
    block_in = jnp.where(section_zero, latents, incoming)
    section_output, saved = forward_block(block_in, pieces, params, bias)
    early, unused = backward_block(cotangent, saved, pieces, params, None, lambda name, v: v)
    returning = lax.ppermute(early, "section", [(1, 0)])
    grad_in = jnp.where(section_zero, returning, cotangent)
    section_output, grad_in = lax.optimization_barrier((section_output, grad_in))
    sums = {}

    shares = {}

    def sink(name, grad, after):
        if name == "feed":
            if whole_tiles:
                grad = feed_weight_grads(*grad, fsdp, fsdp * dp)
            else:
                low, hidden_grad, active, feed_grad = grad
                grad = pack_pieces(
                    *[
                        jnp.einsum("bli,blj->ij", left, right, preferred_element_type=f32)
                        .astype(bf16)
                        .reshape(fsdp * dp, -1, right.shape[-1])
                        for left, right in ((low, hidden_grad), (active, feed_grad))
                    ]
                )
            grad, after = lax.optimization_barrier((grad, after))
            sums["feed"] = lax.psum_scatter(grad, ("fsdp", "dp"), scatter_dimension=0)
            return after
        grad, after = lax.optimization_barrier((grad.astype(bf16), after))
        if name == "outward":
            sums["outward"] = grad
        elif name == "inward":
            sums["inward"] = Reduce([grad, sums["outward"]], fsdp, dp, f, d)
            after = tie(after, sums["inward"].halve())
        return after

    input_gradient, grads = backward_block(
        grad_in, saved, pieces, params, sink, lambda name, value: value
    )
    while sums["inward"].bit < sums["inward"].bits:
        got = sums["inward"].halve()
    tail = jnp.concatenate([grads["modulated"].reshape(-1), grads["biases"].astype(bf16)])
    tail = jnp.stack(
        [tail] + [turn(tail.reshape(-1, width), step, fsdp).reshape(-1) for step in range(1, fsdp)]
    )
    tail = tie(tail, got)
    own_part = sums["feed"]
    if whole_tiles:
        far_part = swap(own_part, 1, dp)
        near_parts = [swap(part, 0, dp) for part in (own_part, far_part)]
        places = jnp.stack([d, d ^ 2, d ^ 1, d ^ 3]).astype(jnp.int32)
        shares["widen"], shares["narrow"] = unpack_shares(
            places, [own_part, far_part] + near_parts, width
        )
    else:
        part = lax.all_gather(own_part, "dp", axis=0)
        shares["widen"], shares["narrow"] = (
            share.astype(f32) for share in unpack_pieces(part, width)
        )
    inward_share, outward_share = sums["inward"].finish()

    tail = spread_small(tail.reshape(fsdp, 1, -1, width), dp).reshape(fsdp * dp, -1)
    count = batch * 6 * width
    modulated_grad = tail[:, :count].reshape(everyone, 6 * width)
    bias_grad = jnp.concatenate(
        [
            jnp.sum(modulated_grad.astype(f32), axis=0),
            jnp.sum(tail[:, count:].astype(f32), axis=0),
        ]
    )
    bias_grad = lax.dynamic_slice_in_dim(bias_grad, f * bias_share, bias_share, 0)
    modulation_grad = dot(low_slice, modulated_grad, ((0,), (0,)))
    condition_grad = dot(modulated_grad, modulation[0], ((1,), (1,)))
    count = lax.axis_size("section")
    for step in range(1, count):
        condition_grad += lax.ppermute(
            condition_grad, "section", [(i, (i + step) % count) for i in range(count)]
        )
    gate = jax.nn.sigmoid(condition)
    condition_grad = condition_grad * (gate * (1.0 + condition * (1.0 - gate)))
    condition_grad = condition_grad.reshape(fsdp, dp * batch, slice_width)
    gathered = [condition_grad]
    for step in range(1, fsdp):
        sent = jnp.roll(condition_grad, step, axis=0)
        gathered.append(turn(sent, step, fsdp))
    gathered = jnp.stack(gathered)[back]
    gathered = jnp.moveaxis(gathered, 0, 2).reshape(everyone, width)
    table_grad = lax.dot_general(
        onehot.astype(f32), gathered, (((0,), (0,)), ((), ())), precision=lax.Precision.HIGHEST
    )
    return (
        section_output[None],
        input_gradient[None],
        modulation_grad[None],
        inward_share[None],
        outward_share[None],
        shares["widen"][None],
        shares["narrow"][None],
        bias_grad[None],
        table_grad,
    )


def solution(mesh):
    return jax.shard_map(
        per_device,
        mesh=mesh,
        in_specs=(
            P(("fsdp", "dp"), None, None),
            P(("fsdp", "dp"), None, None),
            P(("fsdp", "dp")),
            P(("fsdp", "dp")),
            P("section", "fsdp", None),
            P("section", "fsdp", None),
            P("section", "fsdp", None),
            P("section", "fsdp", None),
            P("section", "fsdp", None),
            P("section", "fsdp"),
            P("fsdp", None),
        ),
        out_specs=(
            P("section", ("fsdp", "dp"), None, None),
            P("section", ("fsdp", "dp"), None, None),
            P("section", "fsdp", None),
            P("section", "fsdp", None),
            P("section", "fsdp", None),
            P("section", "fsdp", None),
            P("section", "fsdp", None),
            P("section", "fsdp"),
            P("fsdp", None),
        ),
        check_vma=False,
    )
```

```python
import math

import jax
import jax.numpy as jnp
from jax import lax
from jax.experimental import pallas as pl
from jax.experimental.pallas import tpu as pltpu
from jax.sharding import PartitionSpec as P

HEADS = 12

eps = 1e-06
f32 = jnp.float32
bf16 = jnp.bfloat16


def dot(left, right, dims):
    return lax.dot_general(left, right, (dims, ((), ())), preferred_element_type=f32)


def normalize(values):
    average = jnp.mean(values, axis=-1, keepdims=True)
    centred = values - average
    variance = jnp.mean(centred * centred, axis=-1, keepdims=True)
    inverse = lax.rsqrt(variance + eps)
    return (centred * inverse, inverse)


def normal_back(grad_normed, normed, inverse):
    first_mean = jnp.mean(grad_normed, axis=-1, keepdims=True)
    cross_mean = jnp.mean(grad_normed * normed, axis=-1, keepdims=True)
    return inverse * (grad_normed - first_mean - normed * cross_mean)


def timestep_features(step_ids, model_width):
    half_width = model_width // 2
    frequencies = jnp.exp(
        -math.log(10000.0) * jnp.arange(half_width, dtype=f32) / half_width
    )
    angles = step_ids[:, None] * frequencies[None, :]
    return jnp.concatenate([jnp.cos(angles), jnp.sin(angles)], axis=-1)


def gelu_and_slope(hidden):
    c = math.sqrt(2.0 / math.pi)
    squared = hidden * hidden
    t = jnp.tanh(c * hidden * (1.0 + 0.044715 * squared))
    value = 0.5 * hidden * (1.0 + t)
    slope = 0.5 * (1.0 + t) + 0.5 * hidden * (1.0 - t * t) * c * (1.0 + 3 * 0.044715 * squared)
    return value, slope


PAIR = 2


def pair_columns(ref, part, pair, lanes, width):
    return ref[0, :, part * width + pair * lanes : part * width + (pair + 1) * lanes]


def soft_rows(query, key, factor):
    scores = dot(query, key, ((1,), (1,))) * factor
    raised = jnp.exp(scores - jnp.max(scores, axis=-1, keepdims=True))
    return raised / jnp.sum(raised, axis=-1, keepdims=True)


def attention(projected):
    batch, length, width = projected.shape[0], projected.shape[1], projected.shape[2] // 3
    head = width // HEADS
    lanes = PAIR * head

    def kernel(in_ref, out_ref):
        owner = lax.broadcasted_iota(jnp.int32, (length, lanes), 1) // head
        for pair in range(HEADS // PAIR):
            q, k, v = (pair_columns(in_ref, part, pair, lanes, width) for part in range(3))
            out = jnp.zeros((length, lanes), f32)
            for i in range(PAIR):
                soft = soft_rows(jnp.where(owner == i, q, 0), k, head ** (-0.5))
                out = jnp.where(owner == i, dot(soft.astype(bf16), v, ((1,), (0,))), out)
            out_ref[0, :, pair * lanes : (pair + 1) * lanes] = out.astype(bf16)

    return pl.pallas_call(
        kernel,
        grid=(batch,),
        in_specs=[pl.BlockSpec((1, length, 3 * width), lambda b: (b, 0, 0))],
        out_specs=pl.BlockSpec((1, length, width), lambda b: (b, 0, 0)),
        out_shape=jax.ShapeDtypeStruct((batch, length, width), bf16),
        compiler_params=pltpu.CompilerParams(vmem_limit_bytes=40 * 1024 * 1024),
        cost_estimate=pl.CostEstimate(
            flops=4 * batch * length * length * width,
            bytes_accessed=8 * batch * length * width,
            transcendentals=batch * HEADS * length * length,
        ),
    )(projected)


def attention_back(projected, grad):
    batch, length, width = grad.shape
    head = width // HEADS
    lanes = PAIR * head
    factor = head ** (-0.5)

    def kernel(in_ref, grad_ref, out_ref):
        owner = lax.broadcasted_iota(jnp.int32, (length, lanes), 1) // head
        for pair in range(HEADS // PAIR):
            q, k, v = (pair_columns(in_ref, part, pair, lanes, width) for part in range(3))
            g = pair_columns(grad_ref, 0, pair, lanes, width)
            outs = [jnp.zeros((length, lanes), f32)] * 3
            for i in range(PAIR):
                soft = soft_rows(jnp.where(owner == i, q, 0), k, factor)
                weight = dot(jnp.where(owner == i, g, 0), v, ((1,), (1,)))
                centre = jnp.sum(weight * soft, axis=-1, keepdims=True)
                score = (soft * (weight - centre)).astype(bf16)
                made = (
                    dot(score, k, ((1,), (0,))) * factor,
                    dot(score, q, ((0,), (0,))) * factor,
                    dot(soft.astype(bf16), g, ((0,), (0,))),
                )
                outs = [jnp.where(owner == i, new, old) for new, old in zip(made, outs)]
            for part in range(3):
                begin = part * width + pair * lanes
                out_ref[0, :, begin : begin + lanes] = outs[part].astype(bf16)

    return pl.pallas_call(
        kernel,
        grid=(batch,),
        in_specs=[
            pl.BlockSpec((1, length, 3 * width), lambda b: (b, 0, 0)),
            pl.BlockSpec((1, length, width), lambda b: (b, 0, 0)),
        ],
        out_specs=pl.BlockSpec((1, length, 3 * width), lambda b: (b, 0, 0)),
        out_shape=jax.ShapeDtypeStruct((batch, length, 3 * width), bf16),
        compiler_params=pltpu.CompilerParams(vmem_limit_bytes=40 * 1024 * 1024),
        cost_estimate=pl.CostEstimate(
            flops=10 * batch * length * length * width,
            bytes_accessed=14 * batch * length * width,
            transcendentals=batch * HEADS * length * length,
        ),
    )(projected, grad)


def feed_forward(low, widen, first_bias, narrow):
    batch, length, width = low.shape
    rows, units = batch * length, widen.shape[1]
    tile = 512

    def kernel(low_ref, widen_ref, bias_ref, narrow_ref, active_ref, slope_ref, feed_ref):
        hidden = dot(low_ref[...], widen_ref[...], ((1,), (0,))) + bias_ref[...]
        value, slope = gelu_and_slope(hidden)
        active = value.astype(bf16)
        active_ref[...] = active
        slope_ref[...] = slope.astype(bf16)
        part = dot(active, narrow_ref[...], ((1,), (0,)))

        @pl.when(pl.program_id(0) == 0)
        def _():
            feed_ref[...] = part

        @pl.when(pl.program_id(0) > 0)
        def _():
            feed_ref[...] += part

    active, slope, feed = pl.pallas_call(
        kernel,
        grid=(units // tile,),
        in_specs=[
            pl.BlockSpec((rows, width), lambda j: (0, 0)),
            pl.BlockSpec((width, tile), lambda j: (0, j)),
            pl.BlockSpec((1, tile), lambda j: (0, j)),
            pl.BlockSpec((tile, width), lambda j: (j, 0)),
        ],
        out_specs=[
            pl.BlockSpec((rows, tile), lambda j: (0, j)),
            pl.BlockSpec((rows, tile), lambda j: (0, j)),
            pl.BlockSpec((rows, width), lambda j: (0, 0)),
        ],
        out_shape=[
            jax.ShapeDtypeStruct((rows, units), bf16),
            jax.ShapeDtypeStruct((rows, units), bf16),
            jax.ShapeDtypeStruct((rows, width), f32),
        ],
        compiler_params=pltpu.CompilerParams(vmem_limit_bytes=48 * 1024 * 1024),
        cost_estimate=pl.CostEstimate(
            flops=4 * rows * width * units,
            bytes_accessed=4 * width * units + 4 * rows * units + 6 * rows * width,
            transcendentals=rows * units,
        ),
    )(low.reshape(rows, width), widen, first_bias[None], narrow)
    return (
        active.reshape(batch, length, units),
        slope.reshape(batch, length, units),
        feed.reshape(batch, length, width),
    )


def pack_pieces(widen_rows, narrow_rows):
    count, share, units = widen_rows.shape
    width = narrow_rows.shape[-1]
    beside = narrow_rows.reshape(count, units // width, share, width)
    beside = jnp.swapaxes(beside, 1, 2).reshape(count, share, units)
    return jnp.concatenate([widen_rows, beside], axis=1)


def unpack_pieces(packed, width):
    count, double, units = packed.shape
    share = double // 2
    narrow_rows = packed[:, share:].reshape(count, share, units // width, width)
    narrow_rows = jnp.swapaxes(narrow_rows, 1, 2).reshape(-1, width)
    return packed[:, :share].reshape(-1, units), narrow_rows


def first_feed_forward(low, packed, first_bias, ways):
    batch, length, width = low.shape
    count, double, units = packed.shape
    rows, share, tile, group = batch * length, double // 2, units // ways, count // ways
    side = units // width

    def kernel(low_ref, widen_ref, narrow_ref, bias_ref, widen_out, narrow_out, feed_ref):
        widen = widen_ref[...].reshape(width, tile)
        parts = [narrow_ref[:, :, r * width : (r + 1) * width] for r in range(side)]
        narrow = jnp.stack(parts, axis=1).reshape(tile, width)
        widen_out[...] = widen
        narrow_out[...] = narrow
        hidden = dot(low_ref[...], widen, ((1,), (0,))) + bias_ref[...]
        active = gelu_and_slope(hidden)[0].astype(bf16)
        part = dot(active, narrow, ((1,), (0,)))

        @pl.when(pl.program_id(0) == 0)
        def _():
            feed_ref[...] = part

        @pl.when(pl.program_id(0) > 0)
        def _():
            feed_ref[...] += part

    widen, narrow, feed = pl.pallas_call(
        kernel,
        grid=(ways,),
        in_specs=[
            pl.BlockSpec((rows, width), lambda j: (0, 0)),
            pl.BlockSpec((count, share, tile), lambda j: (0, 0, j)),
            pl.BlockSpec((group, share, units), lambda j: (j, 1, 0)),
            pl.BlockSpec((1, tile), lambda j: (0, j)),
        ],
        out_specs=[
            pl.BlockSpec((width, tile), lambda j: (0, j)),
            pl.BlockSpec((tile, width), lambda j: (j, 0)),
            pl.BlockSpec((rows, width), lambda j: (0, 0)),
        ],
        out_shape=[
            jax.ShapeDtypeStruct((width, units), bf16),
            jax.ShapeDtypeStruct((units, width), bf16),
            jax.ShapeDtypeStruct((rows, width), f32),
        ],
        compiler_params=pltpu.CompilerParams(vmem_limit_bytes=48 * 1024 * 1024),
        cost_estimate=pl.CostEstimate(
            flops=4 * rows * width * units,
            bytes_accessed=8 * width * units + 6 * rows * width,
            transcendentals=rows * units,
        ),
    )(low.reshape(rows, width), packed, packed, first_bias[None])
    return widen, narrow, feed.reshape(batch, length, width)


def feed_weight_grads(low, hidden_grad, active, feed_grad, ways, count):
    width, units = low.shape[-1], active.shape[-1]
    rows = low.shape[0] * low.shape[1]
    share, group, tile, side = width // count, count // ways, units // ways, units // width

    def kernel(low_ref, hidden_ref, active_ref, feed_ref, out_ref):
        widen = dot(low_ref[...], hidden_ref[...], ((1,), (0,))).astype(bf16)
        out_ref[:, :share, :] = widen.reshape(group, share, units)
        narrow = dot(active_ref[...], feed_ref[...], ((0,), (0,))).astype(bf16)
        narrow = narrow.reshape(group, side, share, width)
        for r in range(side):
            out_ref[:, share:, r * width : (r + 1) * width] = narrow[:, r]

    return pl.pallas_call(
        kernel,
        grid=(ways,),
        in_specs=[
            pl.BlockSpec((width // ways, rows), lambda j: (j, 0)),
            pl.BlockSpec((rows, units), lambda j: (0, 0)),
            pl.BlockSpec((rows, tile), lambda j: (0, j)),
            pl.BlockSpec((rows, width), lambda j: (0, 0)),
        ],
        out_specs=pl.BlockSpec((group, 2 * share, units), lambda j: (j, 0, 0)),
        out_shape=jax.ShapeDtypeStruct((count, 2 * share, units), bf16),
        compiler_params=pltpu.CompilerParams(vmem_limit_bytes=48 * 1024 * 1024),
        cost_estimate=pl.CostEstimate(
            flops=4 * rows * width * units,
            bytes_accessed=4 * width * units + 4 * rows * (width + units),
            transcendentals=0,
        ),
    )(
        low.reshape(rows, width).T,
        hidden_grad.reshape(rows, units),
        active.reshape(rows, units),
        feed_grad.reshape(rows, width),
    )


def unpack_shares(place, pieces, width):
    count = len(pieces)
    double, units = pieces[0].shape
    share, side = double // 2, units // width

    def kernel(place_ref, *refs):
        widen_ref, narrow_ref = refs[count:]
        for number in range(count):
            at = place_ref[number]
            rows = pl.ds(pl.multiple_of(at * share, 8), share)
            widen_ref[rows, :] = refs[number][:share, :].astype(f32)
            for r in range(side):
                rows = pl.ds(pl.multiple_of((at * side + r) * share, 8), share)
                part = refs[number][share:, r * width : (r + 1) * width]
                narrow_ref[rows, :] = part.astype(f32)

    whole = pl.BlockSpec(memory_space=pltpu.VMEM)
    return pl.pallas_call(
        kernel,
        in_specs=[pl.BlockSpec(memory_space=pltpu.SMEM)] + [whole] * count,
        out_specs=[whole, whole],
        out_shape=[
            jax.ShapeDtypeStruct((count * share, units), f32),
            jax.ShapeDtypeStruct((count * side * share, width), f32),
        ],
        compiler_params=pltpu.CompilerParams(vmem_limit_bytes=40 * 1024 * 1024),
    )(place, *pieces)


def forward_block(x_in, pieces, params, bias, run_feed=None):
    inward, outward, widen, narrow = params
    batch, length, width = x_in.shape
    x = x_in.astype(f32)
    first_norm, first_inverse = normalize(x)
    first_low = (first_norm * (1.0 + pieces[1][:, None]) + pieces[0][:, None]).astype(bf16)
    projected = (
        jnp.einsum("bli,ij->blj", first_low, inward, preferred_element_type=f32) + bias["in"]
    ).astype(bf16)
    attended = attention(projected)
    branch = jnp.einsum("bli,ij->blj", attended, outward, preferred_element_type=f32) + bias["out"]
    middle = x + pieces[2][:, None] * branch
    second_norm, second_inverse = normalize(middle)
    second_low = (second_norm * (1.0 + pieces[4][:, None]) + pieces[3][:, None]).astype(bf16)
    if run_feed:
        return middle + pieces[5][:, None] * (run_feed(second_low) + bias["ff2"])
    activated, slope, feed = feed_forward(second_low, widen, bias["ff1"], narrow)
    feed = feed + bias["ff2"]
    result = (middle + pieces[5][:, None] * feed).astype(bf16)
    saved = dict(
        x_norm=first_norm, x_inverse=first_inverse, first_low=first_low, projected=projected,
        attended=attended, branch=branch, m_norm=second_norm,
        m_inverse=second_inverse, second_low=second_low, slope=slope,
        activated=activated, feed=feed,
    )
    return result, saved


def backward_block(grad_in, saved, pieces, params, sink, hook):
    inward, outward, widen, narrow = params
    batch, length, width = grad_in.shape
    grad_out = grad_in.astype(f32)
    out = {}

    def weight(a, g):
        return jnp.einsum("bli,blj->ij", a, g, preferred_element_type=f32)

    feed_grad = (pieces[5][:, None] * grad_out).astype(bf16)
    hidden_grad = (
        jnp.einsum("blj,ij->bli", feed_grad, narrow, preferred_element_type=f32)
        * saved["slope"].astype(f32)
    ).astype(bf16)
    if sink:
        operands = (saved["second_low"], hidden_grad, saved["activated"], feed_grad)
        hidden_grad = sink("feed", operands, hidden_grad)
    second_grad = jnp.einsum("blj,ij->bli", hidden_grad, widen, preferred_element_type=f32)
    middle_grad = grad_out + normal_back(
        second_grad * (1.0 + pieces[4][:, None]), saved["m_norm"], saved["m_inverse"]
    )
    attention_grad = (pieces[2][:, None] * middle_grad).astype(bf16)
    if sink:
        attention_grad = sink("outward", weight(saved["attended"], attention_grad), attention_grad)
    attended_grad = jnp.einsum("blj,ij->bli", attention_grad, outward, preferred_element_type=f32)
    attended_grad = hook("attended", attended_grad.astype(bf16))
    projected_grad = attention_back(saved["projected"], attended_grad)
    if sink:
        projected_grad = sink("inward", weight(saved["first_low"], projected_grad), projected_grad)
    first_grad = jnp.einsum("blj,ij->bli", projected_grad, inward, preferred_element_type=f32)
    first_grad = hook("first", first_grad)
    stream = middle_grad + normal_back(
        first_grad * (1.0 + pieces[1][:, None]), saved["x_norm"], saved["x_inverse"]
    )
    if sink:
        total = jnp.sum(projected_grad.astype(f32), axis=(0, 1))
        out["biases"] = jnp.concatenate(
            [
                total[:width],
                total[2 * width :],
                jnp.sum(attention_grad.astype(f32), axis=(0, 1)),
                jnp.sum(hidden_grad.astype(f32), axis=(0, 1)),
                jnp.sum(feed_grad.astype(f32), axis=(0, 1)),
            ]
        )
        out["modulated"] = jnp.concatenate(
            [
                jnp.sum(first_grad, axis=1),
                jnp.sum(first_grad * saved["x_norm"], axis=1),
                jnp.sum(middle_grad * saved["branch"], axis=1),
                jnp.sum(second_grad, axis=1),
                jnp.sum(second_grad * saved["m_norm"], axis=1),
                jnp.sum(grad_out * saved["feed"], axis=1),
            ],
            axis=-1,
        ).astype(bf16)
    return stream.astype(bf16), out


def pick(array, index):
    return lax.dynamic_index_in_dim(array, index, 0, keepdims=False)


def swap(array, bit, count):
    return lax.ppermute(array, "dp", [(i, i ^ (1 << bit)) for i in range(count)])


def turn(array, by, count):
    return lax.ppermute(array, "fsdp", [(i, (i + by) % count) for i in range(count)])


def assemble(place, shards, rounds, far, near, near_far):
    steps = len(rounds)
    share, columns = rounds[0].shape
    parts = far_parts = 4
    ways = steps + 1
    starts, begin = [], 0
    for shard in shards:
        starts.append(begin)
        begin += shard.shape[1]

    def kernel(place_ref, *refs):
        shard_refs = refs[: len(shards)]
        round_refs = refs[len(shards) : len(shards) + steps]
        far_refs = refs[len(shards) + steps : len(shards) + 2 * steps]
        near_refs = refs[len(shards) + 2 * steps : len(shards) + 3 * steps]
        near_far_refs = refs[len(shards) + 3 * steps : len(shards) + 4 * steps]
        outs = refs[len(shards) + 4 * steps :]
        f, d = place_ref[0], place_ref[1]
        core, side = lax.rem(d, 2), lax.div(d, 2)

        def put(out, rows, value):
            out[pl.ds(pl.multiple_of(rows, 16), value.shape[0]), :] = value

        for number, out in enumerate(outs):
            for part in range(parts):
                put(
                    out,
                    (f * parts + part) * share,
                    shard_refs[number][part * share : (part + 1) * share, :],
                )
            begin, end = starts[number], starts[number] + shards[number].shape[1]
            for step in range(steps):
                owner = lax.rem(f + ways - 1 - step, ways)
                base = owner * (parts * share)
                same, other = side * 2 + core, (1 - side) * 2 + core
                put(out, base + same * share, round_refs[step][:, begin:end])
                put(out, base + other * share, far_refs[step][:, begin:end])
                same, other = side * 2 + 1 - core, (1 - side) * 2 + 1 - core
                put(out, base + same * share, near_refs[step][:, begin:end])
                put(out, base + other * share, near_far_refs[step][:, begin:end])

    whole = pl.BlockSpec(memory_space=pltpu.VMEM)
    return pl.pallas_call(
        kernel,
        out_shape=[
            jax.ShapeDtypeStruct((ways * parts * share, shard.shape[1]), bf16) for shard in shards
        ],
        in_specs=[pl.BlockSpec(memory_space=pltpu.SMEM)] + [whole] * (len(shards) + 4 * steps),
        out_specs=[whole] * len(shards),
        compiler_params=pltpu.CompilerParams(vmem_limit_bytes=40 * 1024 * 1024),
    )(place, *shards, *rounds, *far, *near, *near_far)


def tie(value, *others):
    return lax.optimization_barrier((value,) + others)[0]


class Gather:
    def __init__(self, shards, fsdp, dp, f, d):
        self.shards, self.sizes, self.place = shards, (fsdp, dp), (f, d)
        share = shards[0].shape[0] // dp
        own = [lax.dynamic_slice_in_dim(shard, d * share, share, 0) for shard in shards]
        self.plain = dp != 4 or share % 16 != 0 or fsdp == 1
        if self.plain:
            self.outs = [lax.all_gather(o, ("fsdp", "dp"), axis=0, tiled=True) for o in own]
        else:
            self.own = jnp.concatenate(own, axis=1)
            self.rounds, self.far, self.near, self.near_far = [], [], [], []

    def begin(self):
        if not self.plain:
            self.rounds.append(turn(self.own, 1, self.sizes[0]))

    def forward(self):
        if self.plain:
            return self.outs[0]
        fsdp, dp = self.sizes
        last = self.rounds[-1]
        if len(self.rounds) < fsdp - 1:
            self.rounds.append(turn(last, 1, fsdp))
        self.far.append(swap(last, 1, dp))
        self.near.append(swap(last, 0, dp))
        self.near_far.append(swap(self.far[-1], 0, dp))
        return last

    def finish(self):
        if self.plain:
            return self.outs
        while len(self.far) < len(self.rounds):
            self.forward()
        return assemble(
            jnp.stack(self.place), self.shards, self.rounds, self.far, self.near, self.near_far
        )


def gather_small(array, fsdp, dp):
    whole = jnp.stack([array] + [turn(array, step, fsdp) for step in range(1, fsdp)])[:, None]
    return spread_small(whole, dp)


def spread_small(whole, dp):
    for bit in reversed(range(dp.bit_length() - 1)):
        whole = jnp.stack([whole, swap(whole, bit, dp)], axis=2)
        whole = whole.reshape((whole.shape[0], -1) + whole.shape[3:])
    return whole


class Reduce:
    def __init__(self, grads, fsdp, dp, f, d):
        self.sizes, self.place = (fsdp, dp), (f, d)
        self.bits = dp.bit_length() - 1
        self.widths = [grad.shape[1] for grad in grads]
        self.helds = []
        for grad in grads:
            share = grad.shape[0] // (fsdp * dp)
            shape = (fsdp,) + (2,) * self.bits + (share, grad.shape[1])
            self.helds.append(grad.astype(bf16).reshape(shape))
        self.bit = 0
        self.send()

    def part(self, which):
        axis = self.bits - self.bit
        parts = [lax.dynamic_index_in_dim(h, which, axis, keepdims=False) for h in self.helds]
        return jnp.concatenate(parts, -1) if len(parts) > 1 else parts[0]

    def send(self):
        mine = (self.place[1] >> self.bit) & 1
        self.kept = self.part(mine)
        self.sent = self.part(1 - mine)
        self.got = swap(self.sent, self.bit, self.sizes[1])

    def halve(self):
        got = self.got
        held = (self.kept.astype(f32) + got.astype(f32)).astype(bf16)
        self.helds = [held]
        self.bit += 1
        if self.bit < self.bits:
            self.send()
            return got
        fsdp, f = self.sizes[0], self.place[0]
        self.total = [pick(held, f).astype(f32)]
        for step in range(1, fsdp):
            self.total.append(turn(pick(held, lax.rem(f + step, fsdp)), step, fsdp).astype(f32))
        return got

    def finish(self):
        d, dp = self.place[1], self.sizes[1]
        whole = sum(self.total).astype(bf16)[None]
        for bit in reversed(range(self.bits)):
            mine = (d >> bit) & 1
            got = swap(whole, bit, dp)
            low = jnp.where(mine == 0, whole, got)
            high = jnp.where(mine == 0, got, whole)
            whole = jnp.stack([low, high], axis=1).reshape((-1,) + whole.shape[1:])
        whole = whole.reshape((-1, whole.shape[-1])).astype(f32)
        shares, begin = [], 0
        for width in self.widths:
            shares.append(whole[:, begin : begin + width])
            begin += width
        return shares


def per_device(
    latents, cotangent, timesteps, classes,
    modulation, inward, outward, widen, narrow, biases, class_table,
):
    section_zero = lax.axis_index("section") == 0
    fsdp, dp = lax.axis_size("fsdp"), lax.axis_size("dp")
    f, d = lax.axis_index("fsdp"), lax.axis_index("dp")
    batch, length, width = latents.shape
    table_rows = class_table.shape[0]
    slice_width = modulation.shape[1]
    bias_share = biases.shape[1]
    hidden_units = widen.shape[2]
    everyone = fsdp * dp * batch

    def own_piece(shard):
        rows = shard.shape[1] // dp
        return lax.dynamic_slice_in_dim(shard[0], d * rows, rows, 0)

    whole_tiles = dp == 4 and widen.shape[1] % (16 * dp) == 0
    packed = pack_pieces(own_piece(widen)[None], own_piece(narrow)[None])[0]
    packed = lax.all_gather(packed, ("fsdp", "dp"), axis=0)
    chunk = Gather([inward[0], outward[0]], fsdp, dp, f, d)

    own = jnp.concatenate([timesteps.astype(f32), classes.astype(f32), biases[0].astype(f32)])
    if not chunk.plain:
        own = tie(own, chunk.own)
    chunk.begin()
    line = jnp.stack([own] + [turn(own, step, fsdp) for step in range(1, fsdp)])
    line = tie(line, chunk.forward())
    back = lax.rem(f + fsdp - jnp.arange(fsdp), fsdp)
    every_bias = line[:, 2 * batch :][back].reshape(-1)
    labels = f * table_rows + jnp.arange(table_rows, dtype=jnp.int32)

    def onehot_of(ids):
        return (ids.reshape(-1).astype(jnp.int32)[:, None] == labels[None, :]).astype(bf16)

    found = dot(onehot_of(line[:, batch : 2 * batch]), class_table, ((1,), (0,))).astype(bf16)
    found = found.reshape(fsdp, batch, width)

    def columns(index):
        return lax.dynamic_slice_in_dim(found, index * slice_width, slice_width, 2)

    rows = columns(f).astype(f32)
    for step in range(1, fsdp):
        sent = jnp.roll(columns(lax.rem(f + step, fsdp)), step, axis=0)
        rows += turn(sent, step, fsdp).astype(f32)
    features = lax.dynamic_slice_in_dim(
        timestep_features(line[:, :batch].reshape(-1), width), f * slice_width, slice_width, 1
    )
    condition = features.reshape(fsdp, batch, slice_width) + rows
    group = jax.nn.silu(condition).astype(bf16).reshape(fsdp * batch, slice_width)
    group = tie(group, chunk.forward())
    partial = dot(group, modulation[0], ((1,), (0,)))
    partial = tie(partial, chunk.forward())
    partial = partial.reshape(fsdp, batch, -1)
    modulated = partial[0] + every_bias[: 6 * width]
    for step in range(1, fsdp):
        modulated += turn(partial[step], -step, fsdp)
    inward_all, outward_all = chunk.finish()
    params = (inward_all, outward_all, None, None)
    pieces = jnp.split(modulated, 6, axis=-1)
    bias = {
        "in": jnp.concatenate(
            [
                every_bias[6 * width : 7 * width],
                jnp.zeros((width,), f32),
                every_bias[7 * width : 8 * width],
            ]
        ),
        "out": every_bias[8 * width : 9 * width],
        "ff1": every_bias[9 * width : 9 * width + hidden_units],
        "ff2": every_bias[9 * width + hidden_units :],
    }

    weights = []

    def run_feed(low):
        if whole_tiles:
            widen_all, narrow_all, feed = first_feed_forward(low, packed, bias["ff1"], fsdp)
        else:
            widen_all, narrow_all = unpack_pieces(packed, width)
            feed = feed_forward(low, widen_all, bias["ff1"], narrow_all)[2]
        weights.extend([widen_all, narrow_all])
        return feed

    first = forward_block(latents, pieces, params, bias, run_feed).astype(bf16)
    params = (inward_all, outward_all, *weights)
    incoming = lax.ppermute(first, "section", [(0, 1)])
    ids = spread_small(line[:, None, batch : 2 * batch], dp)
    condition = spread_small(condition[:, None], dp).reshape(everyone, slice_width)
    incoming, condition, ids = lax.optimization_barrier((incoming, condition, ids))
    low_slice = jax.nn.silu(condition).astype(bf16)
    onehot = onehot_of(ids)
    block_in = jnp.where(section_zero, latents, incoming)
    section_output, saved = forward_block(block_in, pieces, params, bias)
    early, unused = backward_block(cotangent, saved, pieces, params, None, lambda name, v: v)
    returning = lax.ppermute(early, "section", [(1, 0)])
    grad_in = jnp.where(section_zero, returning, cotangent)
    section_output, grad_in = lax.optimization_barrier((section_output, grad_in))
    sums = {}

    shares = {}

    def sink(name, grad, after):
        if name == "feed":
            if whole_tiles:
                grad = feed_weight_grads(*grad, fsdp, fsdp * dp)
            else:
                low, hidden_grad, active, feed_grad = grad
                grad = pack_pieces(
                    *[
                        jnp.einsum("bli,blj->ij", left, right, preferred_element_type=f32)
                        .astype(bf16)
                        .reshape(fsdp * dp, -1, right.shape[-1])
                        for left, right in ((low, hidden_grad), (active, feed_grad))
                    ]
                )
            grad, after = lax.optimization_barrier((grad, after))
            sums["feed"] = lax.psum_scatter(grad, ("fsdp", "dp"), scatter_dimension=0)
            return after
        grad, after = lax.optimization_barrier((grad.astype(bf16), after))
        if name == "outward":
            sums["outward"] = grad
        elif name == "inward":
            sums["inward"] = Reduce([grad, sums["outward"]], fsdp, dp, f, d)
            sums["inward"].halve()
            after, sums["inward"].kept = lax.optimization_barrier((after, sums["inward"].kept))
            after = tie(after, sums["inward"].sent)
        return after

    input_gradient, grads = backward_block(
        grad_in, saved, pieces, params, sink, lambda name, value: value
    )
    while sums["inward"].bit < sums["inward"].bits:
        got = sums["inward"].halve()
    tail = jnp.concatenate([grads["modulated"].reshape(-1), grads["biases"].astype(bf16)])
    tail = jnp.stack(
        [tail] + [turn(tail.reshape(-1, width), step, fsdp).reshape(-1) for step in range(1, fsdp)]
    )
    tail = tie(tail, got)
    own_part = sums["feed"]
    if whole_tiles:
        far_part = swap(own_part, 1, dp)
        near_parts = [swap(part, 0, dp) for part in (own_part, far_part)]
        places = jnp.stack([d, d ^ 2, d ^ 1, d ^ 3]).astype(jnp.int32)
        shares["widen"], shares["narrow"] = unpack_shares(
            places, [own_part, far_part] + near_parts, width
        )
    else:
        part = lax.all_gather(own_part, "dp", axis=0)
        shares["widen"], shares["narrow"] = (
            share.astype(f32) for share in unpack_pieces(part, width)
        )
    inward_share, outward_share = sums["inward"].finish()

    tail = spread_small(tail.reshape(fsdp, 1, -1, width), dp).reshape(fsdp * dp, -1)
    count = batch * 6 * width
    modulated_grad = tail[:, :count].reshape(everyone, 6 * width)
    bias_grad = jnp.concatenate(
        [
            jnp.sum(modulated_grad.astype(f32), axis=0),
            jnp.sum(tail[:, count:].astype(f32), axis=0),
        ]
    )
    bias_grad = lax.dynamic_slice_in_dim(bias_grad, f * bias_share, bias_share, 0)
    modulation_grad = dot(low_slice, modulated_grad, ((0,), (0,)))
    condition_grad = dot(modulated_grad, modulation[0], ((1,), (1,)))
    count = lax.axis_size("section")
    for step in range(1, count):
        condition_grad += lax.ppermute(
            condition_grad, "section", [(i, (i + step) % count) for i in range(count)]
        )
    gate = jax.nn.sigmoid(condition)
    condition_grad = condition_grad * (gate * (1.0 + condition * (1.0 - gate)))
    condition_grad = condition_grad.reshape(fsdp, dp * batch, slice_width)
    gathered = [condition_grad]
    for step in range(1, fsdp):
        sent = jnp.roll(condition_grad, step, axis=0)
        gathered.append(turn(sent, step, fsdp))
    gathered = jnp.stack(gathered)[back]
    gathered = jnp.moveaxis(gathered, 0, 2).reshape(everyone, width)
    table_grad = lax.dot_general(
        onehot.astype(f32), gathered, (((0,), (0,)), ((), ())), precision=lax.Precision.HIGHEST
    )
    return (
        section_output[None],
        input_gradient[None],
        modulation_grad[None],
        inward_share[None],
        outward_share[None],
        shares["widen"][None],
        shares["narrow"][None],
        bias_grad[None],
        table_grad,
    )


def solution(mesh):
    return jax.shard_map(
        per_device,
        mesh=mesh,
        in_specs=(
            P(("fsdp", "dp"), None, None),
            P(("fsdp", "dp"), None, None),
            P(("fsdp", "dp")),
            P(("fsdp", "dp")),
            P("section", "fsdp", None),
            P("section", "fsdp", None),
            P("section", "fsdp", None),
            P("section", "fsdp", None),
            P("section", "fsdp", None),
            P("section", "fsdp"),
            P("fsdp", None),
        ),
        out_specs=(
            P("section", ("fsdp", "dp"), None, None),
            P("section", ("fsdp", "dp"), None, None),
            P("section", "fsdp", None),
            P("section", "fsdp", None),
            P("section", "fsdp", None),
            P("section", "fsdp", None),
            P("section", "fsdp", None),
            P("section", "fsdp"),
            P("fsdp", None),
        ),
        check_vma=False,
    )
```
